32 devices in a mesh: groups: 2 (over x), space: 16 (over z, y, core).
Axes of the slice: x: 2, y: 2, z: 4, core: 2. Of those that a mesh axis runs over, the one named last changes fastest.
Arguments:
- grid_latent: bfloat16 [65536, 512], P(('groups', 'space')), parts along dimension 0, may hold values from -6 to 6
- mesh_latent: bfloat16 [8192, 512], P(('groups', 'space')), parts along dimension 0, may hold values from -6 to 6
- out_cotangent: bfloat16 [8192, 512], P(('groups', 'space')), parts along dimension 0, may hold values from -6 to 6
- matrices: bfloat16 [2, 4, 512, 512], replicated, may hold values from -0.25 to 0.25
- norm_gains: float32 [2, 512], replicated, may hold values from 0.5 to 1.5
- edge_embeddings: float32 [2, 4, 512], replicated, may hold values from -3 to 3
- enc_attributes: float32 [4, 32768], P(None, 'space'), may hold values from -6 to 6
- proc_attributes: float32 [4, 32768], P(None, 'space'), may hold values from -6 to 6
- enc_send_block: int32 [256], P('space'), may hold values from 0 to 39, as said below
- enc_recv_block: int32 [256], P('space'), may hold values from 0 to 3, as said below
- enc_send_slot: int32 [256, 128], P('space'), may hold values from 0 to 63
- enc_recv_slot: int32 [256, 128], P('space'), may hold values from 0 to 63
- enc_count: int32 [16], P('space'), may hold values from 4 to 16, as said below
- proc_send_block: int32 [256], P('space'), may hold values from 0 to 5, as said below
- proc_recv_block: int32 [256], P('space'), may hold values from 0 to 3, as said below
- proc_send_slot: int32 [256, 128], P('space'), may hold values from 0 to 63
- proc_recv_slot: int32 [256, 128], P('space'), may hold values from 0 to 63
- proc_count: int32 [16], P('space'), may hold values from 4 to 16, as said below
Outputs:
- mesh_out: bfloat16 [8192, 512], P(('groups', 'space')), parts along dimension 0
- grid_grad: bfloat16 [65536, 512], P(('groups', 'space')), parts along dimension 0
- mesh_grad: bfloat16 [8192, 512], P(('groups', 'space')), parts along dimension 0
- matrix_grads: float32 [4, 4, 512, 512], P('groups', None, None, 'space'), parts along dimension 0
- gain_grads: float32 [4, 512], P('groups', 'space'), parts along dimension 0
- embedding_grads: float32 [4, 4, 512], P('groups', None, 'space'), parts along dimension 0
The draws below stay inside these ranges and needn't reach their ends.
There are 2 independent parts, one for each index of `groups`. The reference program is written for one: setup_inputs(seed, part) draws one part's arguments, and reference() takes and returns one part's arrays. A program takes and returns all parts, laid end to end along the dimension named above; an argument that names none is the same for every part. Nothing has to cross between parts.
Inputs may be any that keep to these rules, and one draw needn't show every extreme that they name: `enc_send_block`: counts blocks of 64 of the slab's extended grid rows; the first slab names none before its own rows and the last none after them. `enc_recv_block`: counts blocks of 64 of the slab's own mesh rows. `enc_count`: a multiple of 4; the live blocks come first in the slab's list. `proc_send_block`: counts blocks of 64 of the slab's extended mesh rows; the first slab names none before its own rows and the last none after them. `proc_recv_block`: counts blocks of 64 of the slab's own mesh rows. `proc_count`: a multiple of 4; the live blocks come first in the slab's list.
All inputs are finite; a program needn't handle non-finite values.
Results may differ from the reference program's by a relative error of at most 0.017.
Values may be sent and summed in bfloat16 or wider, within the bound.
A program may use at most 192 MiB of HBM per device.

```python
import jax
import jax.numpy as jnp
from jax import lax

D = 512
BLK = 64
EPB = 128
HG = 256
HM = 64
G_DEV = 2048
M_DEV = 256
NBE = 16
NBP = 16
G = 32768
M = 4096
BLOCKS_ENC = 256
BLOCKS_PROC = 256
EDGES_ENC = 32768
EDGES_PROC = 32768
N_SPACE = 16


def block_lists(key, salt, device_count, blocks_dev, recv_blocks, margin_blocks, ratio):
    key = jax.random.fold_in(key, salt)
    list_shape = (device_count, blocks_dev)
    receiver_nodes = jax.random.randint(key, list_shape, 0, recv_blocks)
    receiver_nodes = receiver_nodes.at[:, 0].set(recv_blocks - 1).at[:, 1].set(0)
    offsets = jax.random.randint(jax.random.fold_in(key, 1), list_shape, -margin_blocks, margin_blocks + ratio)
    sender_nodes = margin_blocks + ratio * receiver_nodes + offsets
    sender_nodes = sender_nodes.at[:, 0].set(2 * margin_blocks + ratio * recv_blocks - 1).at[:, 1].set(0)
    device_row = jnp.arange(device_count)[:, None]
    lowest = jnp.where(device_row == 0, margin_blocks, 0)
    highest = jnp.where(device_row == device_count - 1, margin_blocks + ratio * recv_blocks - 1, 2 * margin_blocks + ratio * recv_blocks - 1)
    sender_nodes = jnp.clip(sender_nodes, lowest, highest)
    return (receiver_nodes.reshape(-1).astype(jnp.int32), sender_nodes.reshape(-1).astype(jnp.int32))


def live_counts(key, device_count, blocks_dev):
    groups = blocks_dev // 4
    live_groups = jax.random.randint(key, (device_count,), 1, (groups + 1) // 2 + 1)
    fullest = jax.random.randint(jax.random.fold_in(key, 1), (), 0, device_count)
    live_groups = jnp.where(jnp.arange(device_count) == fullest, groups, live_groups)
    return (4 * live_groups).astype(jnp.int32)


def draw_enc_recv_block(key, part):
    return block_lists(key, 101, BLOCKS_ENC // NBE, NBE, M_DEV // BLK, HG // BLK, G_DEV // M_DEV)[0]


def draw_enc_send_block(key, part):
    return block_lists(key, 101, BLOCKS_ENC // NBE, NBE, M_DEV // BLK, HG // BLK, G_DEV // M_DEV)[1]


def draw_proc_recv_block(key, part):
    return block_lists(key, 202, BLOCKS_PROC // NBP, NBP, M_DEV // BLK, HM // BLK, 1)[0]


def draw_proc_send_block(key, part):
    return block_lists(key, 202, BLOCKS_PROC // NBP, NBP, M_DEV // BLK, HM // BLK, 1)[1]


def draw_enc_count(key, part):
    key = jax.random.fold_in(key, 7)
    return live_counts(key, BLOCKS_ENC // NBE, NBE)


def draw_proc_count(key, part):
    key = jax.random.fold_in(key, 9)
    return live_counts(key, BLOCKS_PROC // NBP, NBP)


def set_ends(result, own_key, low, largest):
    dims = result.shape
    index_at = [jax.random.randint(jax.random.fold_in(own_key, axis), (), 0, dims[axis]) for axis in range(len(dims))]
    result = result.at[tuple(index_at)].set(low)
    longest = dims.index(max(dims))
    index_at[longest] = (index_at[longest] + 1) % dims[longest]
    return result.at[tuple(index_at)].set(largest)


def shard_levels(rng, extent, shards, smallest, top_value):
    factor_of, own = 1.0, jax.random.fold_in(rng, 6)
    for axis_at, parts in shards:
        steps = jnp.exp(jax.random.uniform(jax.random.fold_in(own, axis_at), (parts,), jnp.float32, smallest / len(shards), top_value / len(shards)))
        factor_of = factor_of * jnp.repeat(steps, extent[axis_at] // parts).reshape([-1 if axis == axis_at else 1 for axis in range(len(extent))])
    return factor_of


def bell_draw(rng, extent, deviation, reach, split=(), kind=jnp.bfloat16):
    entries = jax.random.normal(rng, extent, jnp.float32) * deviation
    if len(split) > 0:
        entries = shard_levels(rng, extent, split, -0.22, 0.18) * entries
    return jnp.clip(entries, min=-reach, max=reach).astype(kind)


def setup_inputs(seed: int = 0, part: int = 0) -> dict:
    key_of = jax.random.split(jax.random.key(seed), 19)
    part_splits = jax.random.split(jax.random.fold_in(key_of[18], part), 19)
    grid_latent = bell_draw(part_splits[0], (G, D), 1.0, 6.0, ((0, 16),))
    mesh_latent = bell_draw(part_splits[1], (M, D), 1.0, 6.0, ((0, 16),))
    out_cotangent = bell_draw(part_splits[2], (M, D), 1.0, 6.0, ((0, 16),))
    matrices = bell_draw(key_of[3], (2, 4, D, D), D ** -0.5, 0.25)
    norm_gains = jnp.clip(1.0 + 0.1 * jax.random.normal(key_of[4], (2, D), jnp.float32), 0.5, 1.5)
    edge_embeddings = bell_draw(key_of[5], (2, 4, D), 4 ** -0.5, 3.0, (), jnp.float32)
    enc_attributes = bell_draw(key_of[6], (4, EDGES_ENC), 1.0, 6.0, ((1, 16),), jnp.float32)
    proc_attributes = bell_draw(key_of[7], (4, EDGES_PROC), 1.0, 6.0, ((1, 16),), jnp.float32)
    enc_send_block = draw_enc_send_block(jax.random.fold_in(key_of[18], 71), part)
    enc_recv_block = draw_enc_recv_block(jax.random.fold_in(key_of[18], 71), part)
    enc_send_slot = set_ends(jax.random.randint(key_of[10], (BLOCKS_ENC, EPB), 0, BLK), jax.random.fold_in(key_of[10], 1), 0, BLK - 1).astype(jnp.int32)
    enc_recv_slot = set_ends(jax.random.randint(key_of[11], (BLOCKS_ENC, EPB), 0, BLK), jax.random.fold_in(key_of[11], 1), 0, BLK - 1).astype(jnp.int32)
    enc_count = draw_enc_count(jax.random.fold_in(key_of[18], 71), part)
    proc_send_block = draw_proc_send_block(jax.random.fold_in(key_of[18], 71), part)
    proc_recv_block = draw_proc_recv_block(jax.random.fold_in(key_of[18], 71), part)
    proc_send_slot = set_ends(jax.random.randint(key_of[15], (BLOCKS_PROC, EPB), 0, BLK), jax.random.fold_in(key_of[15], 1), 0, BLK - 1).astype(jnp.int32)
    proc_recv_slot = set_ends(jax.random.randint(key_of[16], (BLOCKS_PROC, EPB), 0, BLK), jax.random.fold_in(key_of[16], 1), 0, BLK - 1).astype(jnp.int32)
    proc_count = draw_proc_count(jax.random.fold_in(key_of[18], 71), part)
    return dict(grid_latent=grid_latent, mesh_latent=mesh_latent, out_cotangent=out_cotangent, matrices=matrices, norm_gains=norm_gains, edge_embeddings=edge_embeddings, enc_attributes=enc_attributes, proc_attributes=proc_attributes, enc_send_block=enc_send_block, enc_recv_block=enc_recv_block, enc_send_slot=enc_send_slot, enc_recv_slot=enc_recv_slot, enc_count=enc_count, proc_send_block=proc_send_block, proc_recv_block=proc_recv_block, proc_send_slot=proc_send_slot, proc_recv_slot=proc_recv_slot, proc_count=proc_count)


group_blocks = 4
norm_eps = 1e-05

def project(rows_in, matrix):
    return jnp.dot(rows_in, matrix, preferred_element_type=jnp.float32)

def back_project(rows_in, matrix):
    return lax.dot_general(rows_in, matrix, (((1,), (1,)), ((), ())), preferred_element_type=jnp.float32)

def outer_sum(left_rows, right_rows):
    return lax.dot_general(left_rows, right_rows, (((0,), (0,)), ((), ())), preferred_element_type=jnp.float32)

def attribute_term(columns, embedding):
    summed = columns[0][:, None] * embedding[0][None, :]
    for feature in range(1, columns.shape[0]):
        summed = summed + columns[feature][:, None] * embedding[feature][None, :]
    return summed

def select_mesh_tiles(source, starts):

    def one_tile(start_block):
        return lax.dynamic_slice_in_dim(source, start_block * BLK, BLK, 0)
    return jax.vmap(one_tile)(starts)

def one_hot(slots, kind):
    positions = lax.broadcasted_iota(jnp.int32, (1, 1, BLK), 2)
    return (slots[:, :, None] == positions).astype(kind)

def edge_sums(sender_projection, receiver_projection, embedding, attributes, send_block, recv_block, send_slot, recv_slot, live_groups):
    feature_width = receiver_projection.shape[1]
    group_count = send_block.shape[0] // group_blocks

    def active(summed, group_id):
        first_block = group_id * group_blocks
        sender_nodes = lax.dynamic_slice_in_dim(send_block, first_block, group_blocks, 0)
        receiver_nodes = lax.dynamic_slice_in_dim(recv_block, first_block, group_blocks, 0)
        sender_onehot = one_hot(lax.dynamic_slice_in_dim(send_slot, first_block, group_blocks, 0), sender_projection.dtype)
        receiver_onehot = one_hot(lax.dynamic_slice_in_dim(recv_slot, first_block, group_blocks, 0), receiver_projection.dtype)
        pulled_from_sender = jnp.einsum('plx,pxy->ply', sender_onehot, select_mesh_tiles(sender_projection, sender_nodes), preferred_element_type=jnp.float32)
        pulled_from_receiver = jnp.einsum('plx,pxy->ply', receiver_onehot, select_mesh_tiles(receiver_projection, receiver_nodes), preferred_element_type=jnp.float32)
        columns = lax.dynamic_slice_in_dim(attributes, first_block * EPB, group_blocks * EPB, 1)
        preact = pulled_from_sender + pulled_from_receiver + attribute_term(columns, embedding).reshape(group_blocks, EPB, feature_width)
        edge_message_value = jax.nn.silu(preact).astype(receiver_projection.dtype)
        arrived_messages = jnp.einsum('nir,nio->nro', receiver_onehot, edge_message_value, preferred_element_type=jnp.float32)
        for member in range(group_blocks):
            offset = receiver_nodes[member] * BLK
            current = lax.dynamic_slice_in_dim(summed, offset, BLK, 0)
            summed = lax.dynamic_update_slice_in_dim(summed, current + arrived_messages[member], offset, 0)
        return summed

    def skipped(summed, group_id):
        return summed

    def group_step(summed, group_id):
        return (lax.cond(group_id < live_groups, active, skipped, summed, group_id), None)
    initial = jnp.zeros((receiver_projection.shape[0], feature_width), jnp.float32)
    return lax.scan(group_step, initial, jnp.arange(group_count, dtype=jnp.int32))[0]

def node_tail(mixed, latent, norm_gain):
    activated = jax.nn.silu(mixed)
    centred = activated - lax.optimization_barrier(jnp.mean(activated, axis=-1, keepdims=True))
    variance = lax.optimization_barrier(jnp.mean(centred * centred, axis=-1, keepdims=True))
    normed = centred * lax.rsqrt(variance + norm_eps)
    return (latent.astype(jnp.float32) + normed * norm_gain).astype(jnp.bfloat16)

def layer_forward(send_rows, latent, matrices, norm_gain, embedding, attributes, edge_lists, live_groups):
    send_block, recv_block, send_slot, recv_slot = edge_lists
    sender_projection = project(send_rows, matrices[0]).astype(jnp.bfloat16)
    receiver_projection = project(latent, matrices[1]).astype(jnp.bfloat16)
    aggregate = edge_sums(sender_projection, receiver_projection, embedding, attributes, send_block, recv_block, send_slot, recv_slot, live_groups).astype(jnp.bfloat16)
    mixed = project(latent, matrices[2]) + project(aggregate, matrices[3])
    return (node_tail(mixed, latent, norm_gain), (sender_projection, receiver_projection, aggregate, mixed))

def layer_backward(cotangent, send_rows, latent, matrices, norm_gain, embedding, attributes, edge_lists, live_groups, saved):
    sender_projection, receiver_projection, aggregate, mixed = saved
    send_block, recv_block, send_slot, recv_slot = edge_lists
    tail_pull = jax.vjp(node_tail, mixed, latent, norm_gain)[1]
    d_mixed, d_tail, d_gain = tail_pull(cotangent)
    g_mixed = d_mixed.astype(jnp.bfloat16)
    d_aggregate = back_project(g_mixed, matrices[3]).astype(jnp.bfloat16)

    def edges_only(send_part, recv_part, embed_part):
        return edge_sums(send_part, recv_part, embed_part, attributes, send_block, recv_block, send_slot, recv_slot, live_groups)
    edge_pull = jax.vjp(edges_only, sender_projection, receiver_projection, embedding)[1]
    d_send, d_recv, d_embedding = edge_pull(d_aggregate.astype(jnp.float32))
    weight_terms = jnp.stack([outer_sum(send_rows, d_send), outer_sum(latent, d_recv), outer_sum(latent, g_mixed), outer_sum(aggregate, g_mixed)])
    d_send_rows = back_project(d_send, matrices[0]).astype(jnp.bfloat16)
    d_latent = d_tail.astype(jnp.float32) + back_project(g_mixed, matrices[2]) + back_project(d_recv, matrices[1])
    return (d_latent, d_send_rows, weight_terms, d_gain, d_embedding)

def per_device(array):
    return array.reshape((N_SPACE, array.shape[0] // N_SPACE) + array.shape[1:])

def per_device_columns(array):
    return jnp.transpose(array.reshape(array.shape[0], N_SPACE, -1), (1, 0, 2))

def device_rows(padded, device, rows_dev, margin):
    return lax.dynamic_slice_in_dim(padded, device * rows_dev, rows_dev + 2 * margin, 0)

def gather_back(d_latent, d_rows, margin):
    own_rows = d_latent.shape[1]
    upper_rim = d_rows[:, d_rows.shape[1] - margin:]
    lower_rim = d_rows[:, :margin]
    nothing = jnp.zeros_like(upper_rim[:1])
    from_left = jnp.concatenate([nothing, upper_rim[:-1]], 0)
    from_right = jnp.concatenate([lower_rim[1:], nothing], 0)
    summed = d_latent + d_rows[:, margin:margin + own_rows].astype(jnp.float32)
    summed = summed.at[:, :margin].add(from_left.astype(jnp.float32))
    summed = summed.at[:, own_rows - margin:].add(from_right.astype(jnp.float32))
    return summed.astype(jnp.bfloat16)

def reference(grid_latent, mesh_latent, out_cotangent, matrices, norm_gains, edge_embeddings, enc_attributes, proc_attributes, enc_send_block, enc_recv_block, enc_send_slot, enc_recv_slot, enc_count, proc_send_block, proc_recv_block, proc_send_slot, proc_recv_slot, proc_count):
    devices = jnp.arange(N_SPACE, dtype=jnp.int32)
    enc_inputs = (devices, per_device_columns(enc_attributes), per_device(enc_send_block), per_device(enc_recv_block), per_device(enc_send_slot), per_device(enc_recv_slot), enc_count)
    proc_inputs = (devices, per_device_columns(proc_attributes), per_device(proc_send_block), per_device(proc_recv_block), per_device(proc_send_slot), per_device(proc_recv_slot), proc_count)
    grid_padded = jnp.pad(grid_latent, ((HG, HG), (0, 0)))
    mesh_tiles = per_device(mesh_latent)

    def enc_layer(inputs, latent):
        rows_in = device_rows(grid_padded, inputs[0], G_DEV, HG)
        return (rows_in, layer_forward(rows_in, latent, matrices[0], norm_gains[0], edge_embeddings[0], inputs[1], inputs[2:6], inputs[6] // group_blocks))
    enc_out = lax.map(lambda packed: enc_layer(packed[0], packed[1])[1][0], (enc_inputs, mesh_tiles))
    mesh_padded = jnp.pad(enc_out.reshape(-1, enc_out.shape[2]), ((HM, HM), (0, 0)))

    def proc_layer(inputs, latent):
        rows_in = device_rows(mesh_padded, inputs[0], M_DEV, HM)
        return (rows_in, layer_forward(rows_in, latent, matrices[1], norm_gains[1], edge_embeddings[1], inputs[1], inputs[2:6], inputs[6] // group_blocks))
    mesh_out = lax.map(lambda packed: proc_layer(packed[0], packed[1])[1][0], (proc_inputs, enc_out))

    def proc_backward(packed):
        inputs, latent, cotangent = packed
        rows_in, forward = proc_layer(inputs, latent)
        return layer_backward(cotangent, rows_in, latent, matrices[1], norm_gains[1], edge_embeddings[1], inputs[1], inputs[2:6], inputs[6] // group_blocks, forward[1])
    proc_back = lax.map(proc_backward, (proc_inputs, enc_out, per_device(out_cotangent)))
    d_enc_out = gather_back(proc_back[0], proc_back[1], HM)

    def enc_backward(packed):
        inputs, latent, cotangent = packed
        rows_in, forward = enc_layer(inputs, latent)
        return layer_backward(cotangent, rows_in, latent, matrices[0], norm_gains[0], edge_embeddings[0], inputs[1], inputs[2:6], inputs[6] // group_blocks, forward[1])
    enc_back = lax.map(enc_backward, (enc_inputs, mesh_tiles, d_enc_out))
    grid_grad = gather_back(jnp.zeros((N_SPACE, G_DEV, D), jnp.float32), enc_back[1], HG)
    mesh_grad = enc_back[0].astype(jnp.bfloat16).reshape(-1, D)
    matrix_grads = jnp.stack([lax.optimization_barrier(jnp.sum(enc_back[2], 0)), lax.optimization_barrier(jnp.sum(proc_back[2], 0))])
    gain_grads = jnp.stack([lax.optimization_barrier(jnp.sum(enc_back[3], 0)), lax.optimization_barrier(jnp.sum(proc_back[3], 0))])
    embedding_grads = jnp.stack([lax.optimization_barrier(jnp.sum(enc_back[4], 0)), lax.optimization_barrier(jnp.sum(proc_back[4], 0))])
    return (mesh_out.reshape(-1, D), grid_grad.reshape(-1, D), mesh_grad, matrix_grads, gain_grads, embedding_grads)
```

```python
import functools

import jax
import jax.numpy as jnp
from jax import lax
from jax.experimental import pallas as pl
from jax.experimental.pallas import tpu as pltpu
from jax.sharding import PartitionSpec as P

BLK = 64
EPB = 128
HG = 256
HM = 64
GB = 4
GE = GB * EPB
EPS = 1e-05
SMALL = 128
VMEM_LIMIT = 56 * 1024 * 1024

f32 = jnp.float32
bf16 = jnp.bfloat16


def dot(a, b):
    return jnp.dot(a, b, preferred_element_type=f32)


def dot_tb(a, b):
    return lax.dot_general(a, b, (((1,), (1,)), ((), ())), preferred_element_type=f32)


def dot_ta(a, b):
    return lax.dot_general(a, b, (((0,), (0,)), ((), ())), preferred_element_type=f32)


def one_hot_pull(columns, group, base, width):
    lanes = lax.broadcasted_iota(jnp.int32, (EPB, width), 1)
    parts = []
    for m in range(GB):
        b = group * GB + m
        parts.append((lanes == columns[:, b : b + 1] + base[m]).astype(f32).astype(bf16))
    return jnp.concatenate(parts, axis=0)


def one_hot_push(slots_ref, group, base, width):
    rows = lax.broadcasted_iota(jnp.int32, (width, EPB), 0)
    parts = []
    for m in range(GB):
        b = group * GB + m
        parts.append((rows == slots_ref[b : b + 1, :] + base[m]).astype(f32).astype(bf16))
    return jnp.concatenate(parts, axis=1)


SEND_BASE = [m * BLK for m in range(GB)]


def recv_base(recv_block, group):
    return [recv_block[group * GB + m] * BLK for m in range(GB)]


def edges_forward(group, send_tiles, recv_proj, cols_s, cols_r, recv_slot, recv_block, attr, emb):
    base = recv_base(recv_block, group)
    width = recv_proj.shape[0]
    pre = dot(one_hot_pull(cols_s, group, SEND_BASE, GB * BLK), send_tiles)
    pre = pre + dot(one_hot_pull(cols_r, group, base, width), recv_proj)
    pre = pre + dot_ta(attr[:, group * GE : (group + 1) * GE], emb)
    gate = 0.5 * jnp.tanh(0.5 * pre) + 0.5
    act = pre * gate
    slope = gate + act * (1.0 - gate)
    summed = dot(one_hot_push(recv_slot, group, base, width), act.astype(bf16))
    return summed, slope.astype(bf16)


def edges_backward(group, d_agg, slope, cols_r, send_slot, recv_slot, recv_block, attr):
    base = recv_base(recv_block, group)
    width = d_agg.shape[0]
    d_pre = dot(one_hot_pull(cols_r, group, base, width), d_agg) * slope.astype(f32)
    d_pre = d_pre.astype(bf16)
    d_send = dot(one_hot_push(send_slot, group, SEND_BASE, GB * BLK), d_pre)
    d_recv = dot(one_hot_push(recv_slot, group, base, width), d_pre)
    d_emb = dot(attr[:, group * GE : (group + 1) * GE], d_pre)
    return d_send, d_recv, d_emb


def tail_forward(mixed, latent, gain):
    u = mixed * (0.5 * jnp.tanh(0.5 * mixed) + 0.5)
    c = u - jnp.mean(u, axis=-1, keepdims=True)
    v = jnp.mean(c * c, axis=-1, keepdims=True)
    return (latent.astype(f32) + c * lax.rsqrt(v + EPS) * gain).astype(bf16)


def tail_backward(mixed, cot, gain):
    s = 0.5 * jnp.tanh(0.5 * mixed) + 0.5
    u = mixed * s
    c = u - jnp.mean(u, axis=-1, keepdims=True)
    r = lax.rsqrt(jnp.mean(c * c, axis=-1, keepdims=True) + EPS)
    n = c * r
    d_gain = jnp.sum(cot * n, axis=0, keepdims=True)
    dn = cot * gain
    du = r * (dn - jnp.mean(dn, axis=-1, keepdims=True) - n * jnp.mean(dn * n, axis=-1, keepdims=True))
    return (du * (s + u * (1.0 - s))).astype(bf16), d_gain


def write_small(w_ref, d_emb, d_gain):
    width = d_emb.shape[1]
    pad = jnp.zeros((SMALL - 16 - 8, width), f32)
    block = jnp.concatenate([d_emb, jnp.broadcast_to(d_gain, (8, width)), pad], axis=0)
    w_ref[:, 4 * width :] = block.T.astype(bf16)


def enc_forward_kernel(
    send_block, recv_block, count, own, lo, hi, latent, w, gains, emb, attr, send_slot, recv_slot,
    out, agg_out, mixed_out, slope_out, tiles_out, ext, acc, sems,
):
    rows = own.shape[0]
    copies = [
        pltpu.make_async_copy(own, ext.at[pl.ds(HG, rows)], sems.at[0]),
        pltpu.make_async_copy(lo, ext.at[pl.ds(0, HG)], sems.at[1]),
        pltpu.make_async_copy(hi, ext.at[pl.ds(HG + rows, HG)], sems.at[2]),
    ]
    for c in copies:
        c.start()
    recv_proj = dot(latent[...], w[0, 1]).astype(bf16)
    cols_s = send_slot[...].T
    cols_r = recv_slot[...].T
    acc[...] = jnp.zeros_like(acc)
    for c in copies:
        c.wait()
    for group in range(send_slot.shape[0] // GB):

        @pl.when(group * GB < count[0])
        def _(group=group):
            for m in range(GB):
                at = group * GB + m
                start = pl.multiple_of(send_block[at] * BLK, BLK)
                tiles_out[at * BLK : (at + 1) * BLK, :] = ext[pl.ds(start, BLK), :]
            tiles = tiles_out[group * GB * BLK : (group + 1) * GB * BLK, :]
            send_proj = dot(tiles, w[0, 0]).astype(bf16)
            summed, slope = edges_forward(
                group, send_proj, recv_proj, cols_s, cols_r, recv_slot, recv_block, attr, emb[0]
            )
            slope_out[group * GE : (group + 1) * GE, :] = slope
            acc[...] += summed

    agg = acc[...].astype(bf16)
    agg_out[...] = agg
    mixed = dot(latent[...], w[0, 2]) + dot(agg, w[0, 3])
    mixed_out[...] = mixed
    out[...] = tail_forward(mixed, latent[...], gains[0:1, :])


def proc_kernel(
    send_block, recv_block, count, enc_out, lo, hi, cot, w, gains, emb, attr, send_slot, recv_slot,
    out, d_latent, rim_lo, rim_hi, w_out, ext, proj, slopes, acc, d_send_acc, d_emb_acc,
):
    rows, width = enc_out.shape
    groups = send_slot.shape[0] // GB
    latent = enc_out[...]
    ext[0:HM, :] = lo[...]
    ext[HM : HM + rows, :] = latent
    ext[HM + rows :, :] = hi[...]
    proj[...] = dot(ext[...], w[0, 0]).astype(bf16)
    recv_proj = dot(latent, w[0, 1]).astype(bf16)
    cols_s = send_slot[...].T
    cols_r = recv_slot[...].T
    acc[...] = jnp.zeros_like(acc)
    for group in range(groups):

        @pl.when(group * GB < count[0])
        def _(group=group):
            tiles = [
                proj[pl.ds(pl.multiple_of(send_block[group * GB + m] * BLK, BLK), BLK), :]
                for m in range(GB)
            ]
            summed, slope = edges_forward(
                group, jnp.concatenate(tiles, axis=0), recv_proj, cols_s, cols_r, recv_slot,
                recv_block, attr, emb[0],
            )
            slopes[group * GE : (group + 1) * GE, :] = slope
            acc[...] += summed

    agg = acc[...].astype(bf16)
    mixed = dot(latent, w[0, 2]) + dot(agg, w[0, 3])
    out[...] = tail_forward(mixed, latent, gains[1:2, :])

    cot32 = cot[...].astype(f32)
    g, d_gain = tail_backward(mixed, cot32, gains[1:2, :])
    d_agg = dot_tb(g, w[0, 3]).astype(bf16)
    acc[...] = jnp.zeros_like(acc)
    d_send_acc[...] = jnp.zeros_like(d_send_acc)
    d_emb_acc[...] = jnp.zeros_like(d_emb_acc)
    for group in range(groups):

        @pl.when(group * GB < count[0])
        def _(group=group):
            d_send, d_recv, d_emb = edges_backward(
                group, d_agg, slopes[group * GE : (group + 1) * GE, :], cols_r, send_slot,
                recv_slot, recv_block, attr,
            )
            for m in range(GB):
                start = pl.multiple_of(send_block[group * GB + m] * BLK, BLK)
                d_send_acc[pl.ds(start, BLK), :] += d_send[m * BLK : (m + 1) * BLK, :]
            acc[...] += d_recv
            d_emb_acc[...] += d_emb

    d_send = d_send_acc[...].astype(bf16)
    d_recv = acc[...].astype(bf16)
    d_rows = dot_tb(d_send, w[0, 0])
    rim_lo[...] = d_rows[0:HM, :].astype(bf16)
    rim_hi[...] = d_rows[HM + rows :, :].astype(bf16)
    d_latent[...] = (
        cot32 + dot_tb(g, w[0, 2]) + dot_tb(d_recv, w[0, 1]) + d_rows[HM : HM + rows, :]
    )
    w_out[:, 0:width] = dot_ta(d_send, ext[...]).astype(bf16)
    w_out[:, width : 2 * width] = dot_ta(d_recv, latent).astype(bf16)
    w_out[:, 2 * width : 3 * width] = dot_ta(g, latent).astype(bf16)
    w_out[:, 3 * width : 4 * width] = dot_ta(g, agg).astype(bf16)
    write_small(w_out, d_emb_acc[...], d_gain)


def enc_backward_kernel(
    send_block, recv_block, count, d_latent, back_lo, back_hi, latent, agg, mixed, slopes, tiles,
    w, gains, attr, send_slot, recv_slot,
    mesh_grad, grid_own, grid_lo, grid_hi, w_out, grid_acc, acc, d_emb_acc, w0_acc, cot_ref,
):
    rows, width = latent.shape
    groups = send_slot.shape[0] // GB
    cot_ref[...] = d_latent[...]
    cot_ref[0:HM, :] += back_lo[...].astype(f32)
    cot_ref[rows - HM :, :] += back_hi[...].astype(f32)
    cot = cot_ref[...].astype(bf16).astype(f32)
    g, d_gain = tail_backward(mixed[...], cot, gains[0:1, :])
    d_agg = dot_tb(g, w[0, 3]).astype(bf16)
    cols_r = recv_slot[...].T
    grid_acc[...] = jnp.zeros_like(grid_acc)
    acc[...] = jnp.zeros_like(acc)
    d_emb_acc[...] = jnp.zeros_like(d_emb_acc)
    w0_acc[...] = jnp.zeros_like(w0_acc)
    for group in range(groups):

        @pl.when(group * GB < count[0])
        def _(group=group):
            d_send, d_recv, d_emb = edges_backward(
                group, d_agg, slopes[group * GE : (group + 1) * GE, :], cols_r, send_slot,
                recv_slot, recv_block, attr,
            )
            d_send = d_send.astype(bf16)
            d_rows = dot_tb(d_send, w[0, 0])
            for m in range(GB):
                start = pl.multiple_of(send_block[group * GB + m] * BLK, BLK)
                grid_acc[pl.ds(start, BLK), :] += d_rows[m * BLK : (m + 1) * BLK, :]
            acc[...] += d_recv
            d_emb_acc[...] += d_emb
            w0_acc[...] += dot_ta(d_send, tiles[group * GB * BLK : (group + 1) * GB * BLK, :])

    own = grid_own.shape[0]
    grid_lo[...] = grid_acc[0:HG, :].astype(bf16)
    grid_hi[...] = grid_acc[HG + own :, :].astype(bf16)
    grid_own[...] = grid_acc[HG : HG + own, :].astype(bf16)
    d_recv = acc[...].astype(bf16)
    mesh_grad[...] = (cot + dot_tb(g, w[0, 2]) + dot_tb(d_recv, w[0, 1])).astype(bf16)
    w_out[:, 0:width] = w0_acc[...].astype(bf16)
    w_out[:, width : 2 * width] = dot_ta(d_recv, latent[...]).astype(bf16)
    w_out[:, 2 * width : 3 * width] = dot_ta(g, latent[...]).astype(bf16)
    w_out[:, 3 * width : 4 * width] = dot_ta(g, agg[...]).astype(bf16)
    write_small(w_out, d_emb_acc[...], d_gain)


smem = pl.BlockSpec(memory_space=pltpu.SMEM)
hbm = pl.BlockSpec(memory_space=pl.ANY)
vmem = pl.BlockSpec(memory_space=pltpu.VMEM)


def layer_spec(layer, shape):
    tail = (0,) * (len(shape) - 1)
    return pl.BlockSpec((1,) + shape[1:], lambda i: (layer,) + tail)


def call(kernel, in_specs, out_shape, scratch, flops):
    return pl.pallas_call(
        kernel,
        grid=(1,),
        in_specs=in_specs,
        out_specs=[vmem] * len(out_shape),
        out_shape=out_shape,
        scratch_shapes=scratch,
        compiler_params=pltpu.CompilerParams(vmem_limit_bytes=VMEM_LIMIT),
        cost_estimate=pl.CostEstimate(flops=flops, bytes_accessed=10_000_000, transcendentals=0),
    )


def shift(up, down, axis):
    ends = lax.axis_size(axis) - 1
    return (
        lax.ppermute(up, axis, [(i, i + 1) for i in range(ends)]),
        lax.ppermute(down, axis, [(i + 1, i) for i in range(ends)]),
    )


def split_rows(a, axis, order):
    top = lax.reduce_precision(a, 8, 7)
    rest = a - top
    pieces = [top if k else rest for k in order]
    return jnp.concatenate(pieces + [jnp.zeros_like(a)], axis=axis).astype(bf16)


def per_device(
    grid_latent, mesh_latent, out_cotangent, matrices, norm_gains, edge_embeddings,
    enc_attributes, proc_attributes, enc_send_block, enc_recv_block, enc_send_slot,
    enc_recv_slot, enc_count, proc_send_block, proc_recv_block, proc_send_slot,
    proc_recv_slot, proc_count,
):
    rows, width = mesh_latent.shape
    own = grid_latent.shape[0]
    blocks = enc_send_block.shape[0]
    p_blocks = proc_send_block.shape[0]
    sds = jax.ShapeDtypeStruct
    emb = split_rows(edge_embeddings, 1, (1, 1, 0))
    enc_attr = split_rows(enc_attributes, 0, (1, 0, 1))
    proc_attr = split_rows(proc_attributes, 0, (1, 0, 1))

    lo, hi = shift(grid_latent[own - HG :], grid_latent[:HG], "space")
    enc_out, agg, mixed, slopes, tiles = call(
        enc_forward_kernel,
        [smem] * 3 + [hbm] * 3 + [vmem, layer_spec(0, matrices.shape), vmem, layer_spec(0, emb.shape), vmem, vmem, vmem],
        [
            sds((rows, width), bf16),
            sds((rows, width), bf16),
            sds((rows, width), f32),
            sds((blocks * EPB, width), bf16),
            sds((blocks * BLK, width), bf16),
        ],
        [
            pltpu.VMEM((own + 2 * HG, width), bf16),
            pltpu.VMEM((rows, width), f32),
            pltpu.SemaphoreType.DMA((3,)),
        ],
        4_000_000_000,
    )(
        enc_send_block, enc_recv_block, enc_count, grid_latent, lo, hi, mesh_latent, matrices,
        norm_gains, emb, enc_attr, enc_send_slot, enc_recv_slot,
    )

    lo, hi = shift(enc_out[rows - HM :], enc_out[:HM], "space")
    mesh_out, d_latent, rim_lo, rim_hi, proc_w = call(
        proc_kernel,
        [smem] * 3 + [vmem] * 4 + [layer_spec(1, matrices.shape), vmem, layer_spec(1, emb.shape), vmem, vmem, vmem],
        [
            sds((rows, width), bf16),
            sds((rows, width), f32),
            sds((HM, width), bf16),
            sds((HM, width), bf16),
            sds((width, 4 * width + SMALL), bf16),
        ],
        [
            pltpu.VMEM((rows + 2 * HM, width), bf16),
            pltpu.VMEM((rows + 2 * HM, width), bf16),
            pltpu.VMEM((p_blocks * EPB, width), bf16),
            pltpu.VMEM((rows, width), f32),
            pltpu.VMEM((rows + 2 * HM, width), f32),
            pltpu.VMEM((16, width), f32),
        ],
        8_000_000_000,
    )(
        proc_send_block, proc_recv_block, proc_count, enc_out, lo, hi, out_cotangent, matrices,
        norm_gains, emb, proc_attr, proc_send_slot, proc_recv_slot,
    )

    back_lo, back_hi = shift(rim_hi, rim_lo, "space")
    proc_sum = lax.psum_scatter(proc_w, "space", scatter_dimension=0, tiled=True)
    mesh_grad, grid_own, grid_lo, grid_hi, enc_w = call(
        enc_backward_kernel,
        [smem] * 3 + [vmem] * 8 + [layer_spec(0, matrices.shape), vmem, vmem, vmem, vmem],
        [
            sds((rows, width), bf16),
            sds((own, width), bf16),
            sds((HG, width), bf16),
            sds((HG, width), bf16),
            sds((width, 4 * width + SMALL), bf16),
        ],
        [
            pltpu.VMEM((own + 2 * HG, width), f32),
            pltpu.VMEM((rows, width), f32),
            pltpu.VMEM((16, width), f32),
            pltpu.VMEM((width, width), f32),
            pltpu.VMEM((rows, width), f32),
        ],
        8_000_000_000,
    )(
        enc_send_block, enc_recv_block, enc_count, d_latent, back_lo, back_hi, mesh_latent, agg,
        mixed, slopes, tiles, matrices, norm_gains, enc_attr, enc_send_slot, enc_recv_slot,
    )
    from_prev, from_next = shift(grid_hi, grid_lo, "space")
    grid_grad = grid_own.at[:HG].add(from_prev).at[own - HG :].add(from_next)
    enc_sum = lax.psum_scatter(enc_w, "space", scatter_dimension=0, tiled=True)

    sums = jnp.stack([enc_sum, proc_sum]).astype(f32)
    columns = sums.shape[1]
    matrix_grads = sums[:, :, : 4 * width].reshape(2, columns, 4, width).transpose(0, 2, 3, 1)
    small = sums[:, :, 4 * width :].transpose(0, 2, 1)
    embedding_grads = small[:, 0:4] + small[:, 4:8]
    gain_grads = small[:, 16]
    return (mesh_out, grid_grad, mesh_grad, matrix_grads, gain_grads, embedding_grads)


def solution(mesh):
    rows = P(("groups", "space"), None)
    lists = (P("space"), P("space"), P("space", None), P("space", None), P("space"))
    return jax.shard_map(
        per_device,
        mesh=mesh,
        in_specs=(rows, rows, rows, P(), P(), P(), P(None, "space"), P(None, "space")) + lists + lists,
        out_specs=(
            rows,
            rows,
            rows,
            P("groups", None, None, "space"),
            P("groups", "space"),
            P("groups", None, "space"),
        ),
        check_vma=False,
    )
```

```python
import functools

import jax
import jax.numpy as jnp
from jax import lax
from jax.experimental import pallas as pl
from jax.experimental.pallas import tpu as pltpu
from jax.sharding import PartitionSpec as P

BLK = 64
EPB = 128
HG = 256
HM = 64
GB = 4
GE = GB * EPB
EPS = 1e-05
SMALL = 128
VMEM_LIMIT = 56 * 1024 * 1024

f32 = jnp.float32
bf16 = jnp.bfloat16


def dot(a, b):
    return jnp.dot(a, b, preferred_element_type=f32)


def dot_tb(a, b):
    return lax.dot_general(a, b, (((1,), (1,)), ((), ())), preferred_element_type=f32)


def dot_ta(a, b):
    return lax.dot_general(a, b, (((0,), (0,)), ((), ())), preferred_element_type=f32)


def one_hot_pull(columns, group, base, width):
    lanes = lax.broadcasted_iota(jnp.int32, (EPB, width), 1)
    parts = []
    for m in range(GB):
        b = group * GB + m
        parts.append((lanes == columns[:, b : b + 1] + base[m]).astype(f32).astype(bf16))
    return jnp.concatenate(parts, axis=0)


def one_hot_push(slots_ref, group, base, width):
    rows = lax.broadcasted_iota(jnp.int32, (width, EPB), 0)
    parts = []
    for m in range(GB):
        b = group * GB + m
        parts.append((rows == slots_ref[b : b + 1, :] + base[m]).astype(f32).astype(bf16))
    return jnp.concatenate(parts, axis=1)


SEND_BASE = [m * BLK for m in range(GB)]


def recv_base(recv_block, group):
    return [recv_block[group * GB + m] * BLK for m in range(GB)]


def edges_forward(group, send_tiles, recv_proj, cols_s, cols_r, recv_slot, recv_block, attr, emb):
    base = recv_base(recv_block, group)
    width = recv_proj.shape[0]
    pre = dot(one_hot_pull(cols_s, group, SEND_BASE, GB * BLK), send_tiles)
    pre = pre + dot(one_hot_pull(cols_r, group, base, width), recv_proj)
    pre = pre + dot_ta(attr[:, group * GE : (group + 1) * GE], emb)
    gate = 0.5 * jnp.tanh(0.5 * pre) + 0.5
    act = pre * gate
    slope = gate + act * (1.0 - gate)
    summed = dot(one_hot_push(recv_slot, group, base, width), act.astype(bf16))
    return summed, slope.astype(bf16)


def edges_backward(group, d_agg, slope, cols_r, send_slot, recv_slot, recv_block, attr):
    base = recv_base(recv_block, group)
    width = d_agg.shape[0]
    d_pre = dot(one_hot_pull(cols_r, group, base, width), d_agg) * slope.astype(f32)
    d_pre = d_pre.astype(bf16)
    d_send = dot(one_hot_push(send_slot, group, SEND_BASE, GB * BLK), d_pre)
    d_recv = dot(one_hot_push(recv_slot, group, base, width), d_pre)
    d_emb = dot(attr[:, group * GE : (group + 1) * GE], d_pre)
    return d_send, d_recv, d_emb


def tail_forward(mixed, latent, gain):
    u = mixed * (0.5 * jnp.tanh(0.5 * mixed) + 0.5)
    c = u - jnp.mean(u, axis=-1, keepdims=True)
    v = jnp.mean(c * c, axis=-1, keepdims=True)
    return (latent.astype(f32) + c * lax.rsqrt(v + EPS) * gain).astype(bf16)


def tail_backward(mixed, cot, gain):
    s = 0.5 * jnp.tanh(0.5 * mixed) + 0.5
    u = mixed * s
    c = u - jnp.mean(u, axis=-1, keepdims=True)
    r = lax.rsqrt(jnp.mean(c * c, axis=-1, keepdims=True) + EPS)
    n = c * r
    d_gain = jnp.sum(cot * n, axis=0, keepdims=True)
    dn = cot * gain
    du = r * (dn - jnp.mean(dn, axis=-1, keepdims=True) - n * jnp.mean(dn * n, axis=-1, keepdims=True))
    return (du * (s + u * (1.0 - s))).astype(bf16), d_gain


def halving_order(parts, layer):
    order = list(range(parts.bit_length() - 1))
    if layer == 0 and len(order) > 2:
        order[1], order[2] = order[2], order[1]
    return order


def shard_at(place, parts, layer):
    order = halving_order(parts, layer)
    slab = 0
    for k, bit in enumerate(order):
        slab += ((place >> (len(order) - 1 - k)) & 1) << bit
    return slab


def write_shards(w_ref, layer, column, value):
    parts, rows, _ = w_ref.shape
    for place in range(parts):
        slab = shard_at(place, parts, layer)
        w_ref[place, :, column : column + value.shape[1]] = value[
            slab * rows : (slab + 1) * rows, :
        ].astype(bf16)


def write_small(w_ref, layer, d_emb, d_gain):
    width = d_emb.shape[1]
    pad = jnp.zeros((SMALL - 16 - 8, width), f32)
    block = jnp.concatenate([d_emb, jnp.broadcast_to(d_gain, (8, width)), pad], axis=0)
    write_shards(w_ref, layer, 4 * width, block.T)


def enc_forward_kernel(
    send_block, recv_block, count, own, lo, hi, latent, w, gains, emb, attr, send_slot, recv_slot,
    out, agg_out, mixed_out, slope_out, tiles_out, ext, acc, sems,
):
    rows = own.shape[0]
    copies = [
        pltpu.make_async_copy(own, ext.at[pl.ds(HG, rows)], sems.at[0]),
        pltpu.make_async_copy(lo, ext.at[pl.ds(0, HG)], sems.at[1]),
        pltpu.make_async_copy(hi, ext.at[pl.ds(HG + rows, HG)], sems.at[2]),
    ]
    for c in copies:
        c.start()
    recv_proj = dot(latent[...], w[0, 1]).astype(bf16)
    cols_s = send_slot[...].T
    cols_r = recv_slot[...].T
    acc[...] = jnp.zeros_like(acc)
    for c in copies:
        c.wait()
    for group in range(send_slot.shape[0] // GB):

        @pl.when(group * GB < count[0])
        def _(group=group):
            for m in range(GB):
                at = group * GB + m
                start = pl.multiple_of(send_block[at] * BLK, BLK)
                tiles_out[at * BLK : (at + 1) * BLK, :] = ext[pl.ds(start, BLK), :]
            tiles = tiles_out[group * GB * BLK : (group + 1) * GB * BLK, :]
            send_proj = dot(tiles, w[0, 0]).astype(bf16)
            summed, slope = edges_forward(
                group, send_proj, recv_proj, cols_s, cols_r, recv_slot, recv_block, attr, emb[0]
            )
            slope_out[group * GE : (group + 1) * GE, :] = slope
            acc[...] += summed

    agg = acc[...].astype(bf16)
    agg_out[...] = agg
    mixed = dot(latent[...], w[0, 2]) + dot(agg, w[0, 3])
    mixed_out[...] = mixed
    out[...] = tail_forward(mixed, latent[...], gains[0:1, :])


def proc_kernel(
    send_block, recv_block, count, enc_out, lo, hi, cot, w, gains, emb, attr, send_slot, recv_slot,
    out, d_latent, rim_lo, rim_hi, w_out, ext, proj, slopes, acc, d_send_acc, d_emb_acc,
):
    rows, width = enc_out.shape
    groups = send_slot.shape[0] // GB
    latent = enc_out[...]
    ext[0:HM, :] = lo[...]
    ext[HM : HM + rows, :] = latent
    ext[HM + rows :, :] = hi[...]
    proj[...] = dot(ext[...], w[0, 0]).astype(bf16)
    recv_proj = dot(latent, w[0, 1]).astype(bf16)
    cols_s = send_slot[...].T
    cols_r = recv_slot[...].T
    acc[...] = jnp.zeros_like(acc)
    for group in range(groups):

        @pl.when(group * GB < count[0])
        def _(group=group):
            tiles = [
                proj[pl.ds(pl.multiple_of(send_block[group * GB + m] * BLK, BLK), BLK), :]
                for m in range(GB)
            ]
            summed, slope = edges_forward(
                group, jnp.concatenate(tiles, axis=0), recv_proj, cols_s, cols_r, recv_slot,
                recv_block, attr, emb[0],
            )
            slopes[group * GE : (group + 1) * GE, :] = slope
            acc[...] += summed

    agg = acc[...].astype(bf16)
    mixed = dot(latent, w[0, 2]) + dot(agg, w[0, 3])
    out[...] = tail_forward(mixed, latent, gains[1:2, :])

    cot32 = cot[...].astype(f32)
    g, d_gain = tail_backward(mixed, cot32, gains[1:2, :])
    d_agg = dot_tb(g, w[0, 3]).astype(bf16)
    acc[...] = jnp.zeros_like(acc)
    d_send_acc[...] = jnp.zeros_like(d_send_acc)
    d_emb_acc[...] = jnp.zeros_like(d_emb_acc)
    for group in range(groups):

        @pl.when(group * GB < count[0])
        def _(group=group):
            d_send, d_recv, d_emb = edges_backward(
                group, d_agg, slopes[group * GE : (group + 1) * GE, :], cols_r, send_slot,
                recv_slot, recv_block, attr,
            )
            for m in range(GB):
                start = pl.multiple_of(send_block[group * GB + m] * BLK, BLK)
                d_send_acc[pl.ds(start, BLK), :] += d_send[m * BLK : (m + 1) * BLK, :]
            acc[...] += d_recv
            d_emb_acc[...] += d_emb

    d_send = d_send_acc[...].astype(bf16)
    d_recv = acc[...].astype(bf16)
    d_rows = dot_tb(d_send, w[0, 0])
    rim_lo[...] = d_rows[0:HM, :].astype(bf16)
    rim_hi[...] = d_rows[HM + rows :, :].astype(bf16)
    d_latent[...] = (
        cot32 + dot_tb(g, w[0, 2]) + dot_tb(d_recv, w[0, 1]) + d_rows[HM : HM + rows, :]
    )
    write_shards(w_out, 1, 0, dot_ta(d_send, ext[...]))
    write_shards(w_out, 1, width, dot_ta(d_recv, latent))
    write_shards(w_out, 1, 2 * width, dot_ta(g, latent))
    write_shards(w_out, 1, 3 * width, dot_ta(g, agg))
    write_small(w_out, 1, d_emb_acc[...], d_gain)


def enc_backward_kernel(
    send_block, recv_block, count, d_latent, back_lo, back_hi, latent, agg, mixed, slopes, tiles,
    w, gains, attr, send_slot, recv_slot,
    mesh_grad, grid_own, grid_lo, grid_hi, w_out, grid_acc, acc, d_emb_acc, w0_acc, cot_ref,
):
    rows, width = latent.shape
    groups = send_slot.shape[0] // GB
    cot_ref[...] = d_latent[...]
    cot_ref[0:HM, :] += back_lo[...].astype(f32)
    cot_ref[rows - HM :, :] += back_hi[...].astype(f32)
    cot = cot_ref[...].astype(bf16).astype(f32)
    g, d_gain = tail_backward(mixed[...], cot, gains[0:1, :])
    d_agg = dot_tb(g, w[0, 3]).astype(bf16)
    cols_r = recv_slot[...].T
    grid_acc[...] = jnp.zeros_like(grid_acc)
    acc[...] = jnp.zeros_like(acc)
    d_emb_acc[...] = jnp.zeros_like(d_emb_acc)
    w0_acc[...] = jnp.zeros_like(w0_acc)
    for group in range(groups):

        @pl.when(group * GB < count[0])
        def _(group=group):
            d_send, d_recv, d_emb = edges_backward(
                group, d_agg, slopes[group * GE : (group + 1) * GE, :], cols_r, send_slot,
                recv_slot, recv_block, attr,
            )
            d_send = d_send.astype(bf16)
            d_rows = dot_tb(d_send, w[0, 0])
            for m in range(GB):
                start = pl.multiple_of(send_block[group * GB + m] * BLK, BLK)
                grid_acc[pl.ds(start, BLK), :] += d_rows[m * BLK : (m + 1) * BLK, :]
            acc[...] += d_recv
            d_emb_acc[...] += d_emb
            w0_acc[...] += dot_ta(d_send, tiles[group * GB * BLK : (group + 1) * GB * BLK, :])

    own = grid_own.shape[0]
    grid_lo[...] = grid_acc[0:HG, :].astype(bf16)
    grid_hi[...] = grid_acc[HG + own :, :].astype(bf16)
    grid_own[...] = grid_acc[HG : HG + own, :].astype(bf16)
    d_recv = acc[...].astype(bf16)
    mesh_grad[...] = (cot + dot_tb(g, w[0, 2]) + dot_tb(d_recv, w[0, 1])).astype(bf16)
    write_shards(w_out, 0, 0, w0_acc[...])
    write_shards(w_out, 0, width, dot_ta(d_recv, latent[...]))
    write_shards(w_out, 0, 2 * width, dot_ta(g, latent[...]))
    write_shards(w_out, 0, 3 * width, dot_ta(g, agg[...]))
    write_small(w_out, 0, d_emb_acc[...], d_gain)


smem = pl.BlockSpec(memory_space=pltpu.SMEM)
hbm = pl.BlockSpec(memory_space=pl.ANY)
vmem = pl.BlockSpec(memory_space=pltpu.VMEM)


def layer_spec(layer, shape):
    tail = (0,) * (len(shape) - 1)
    return pl.BlockSpec((1,) + shape[1:], lambda i: (layer,) + tail)


def call(kernel, in_specs, out_shape, scratch, flops):
    return pl.pallas_call(
        kernel,
        grid=(1,),
        in_specs=in_specs,
        out_specs=[vmem] * len(out_shape),
        out_shape=out_shape,
        scratch_shapes=scratch,
        compiler_params=pltpu.CompilerParams(vmem_limit_bytes=VMEM_LIMIT),
        cost_estimate=pl.CostEstimate(flops=flops, bytes_accessed=10_000_000, transcendentals=0),
    )


def greet(targets):
    barrier = pltpu.get_barrier_semaphore()
    for slab, there in targets:

        @pl.when(there)
        def _(slab=slab):
            pl.semaphore_signal(
                barrier, inc=1, device_id={"space": slab}, device_id_type=pl.DeviceIdType.MESH
            )

    pl.semaphore_wait(barrier, sum(jnp.where(there, 1, 0) for _, there in targets))


def remote(src, dst, send_sem, recv_sem, slab):
    return pltpu.make_async_remote_copy(
        src_ref=src,
        dst_ref=dst,
        send_sem=send_sem,
        recv_sem=recv_sem,
        device_id={"space": slab},
        device_id_type=pl.DeviceIdType.MESH,
    )


def neighbours(parts):
    me = lax.axis_index("space")
    has_prev, has_next = me > 0, me < parts - 1
    return jnp.maximum(me - 1, 0), jnp.minimum(me + 1, parts - 1), has_prev, has_next


def start_halo(parts, up, down, from_prev, from_next, send_sem, recv_sem):
    prev, after, has_prev, has_next = neighbours(parts)

    @pl.when(has_next)
    def _():
        remote(up, from_prev, send_sem.at[0], recv_sem.at[0], after).start()

    @pl.when(has_prev)
    def _():
        remote(down, from_next, send_sem.at[1], recv_sem.at[1], prev).start()

    @pl.when(jnp.logical_not(has_prev))
    def _():
        from_prev[...] = jnp.zeros_like(from_prev)

    @pl.when(jnp.logical_not(has_next))
    def _():
        from_next[...] = jnp.zeros_like(from_next)


def finish_halo(parts, up, down, from_prev, from_next, send_sem, recv_sem):
    prev, after, has_prev, has_next = neighbours(parts)

    @pl.when(has_next)
    def _():
        remote(up, from_prev, send_sem.at[0], recv_sem.at[0], after).wait_send()
        remote(down, from_next, send_sem.at[1], recv_sem.at[1], after).wait_recv()

    @pl.when(has_prev)
    def _():
        remote(down, from_next, send_sem.at[1], recv_sem.at[1], prev).wait_send()
        remote(up, from_prev, send_sem.at[0], recv_sem.at[0], prev).wait_recv()


def exchange_kernel(parts, up, down, from_prev, from_next, send_sem, recv_sem):
    prev, after, has_prev, has_next = neighbours(parts)
    greet([(prev, has_prev), (after, has_next)])
    refs = (up, down, from_prev, from_next, send_sem, recv_sem)
    start_halo(parts, *refs)
    finish_halo(parts, *refs)


def exchange(parts, up, down, width, margin, up_block, down_block, collective_id):
    return pl.pallas_call(
        functools.partial(exchange_kernel, parts),
        grid=(1,),
        in_specs=[
            pl.BlockSpec((margin, width), lambda i: (up_block, 0)),
            pl.BlockSpec((margin, width), lambda i: (down_block, 0)),
        ],
        out_specs=[vmem] * 2,
        out_shape=[jax.ShapeDtypeStruct((margin, width), bf16)] * 2,
        scratch_shapes=[pltpu.SemaphoreType.DMA((2,)), pltpu.SemaphoreType.DMA((2,))],
        compiler_params=pltpu.CompilerParams(collective_id=collective_id, has_side_effects=True),
    )(up, down)


def reduce_kernel(parts, enc_w, proc_w, up, down, enc_out, proc_out, from_prev, from_next, *scratch):
    halo_send, halo_recv, send_sem, recv_sem = scratch[-4:]
    stages = parts.bit_length() - 1
    landing = [scratch[0:stages], scratch[stages : 2 * stages]]
    kept = [scratch[2 * stages : 3 * stages - 1], scratch[3 * stages - 1 : 4 * stages - 2]]
    outs = [enc_out, proc_out]
    current = [enc_w, proc_w]
    me = lax.axis_index("space")

    def bit_of(bit):
        return (me // (1 << bit)) % 2

    prev, after, has_prev, has_next = neighbours(parts)
    greet(
        [(me + (1 - 2 * bit_of(bit)) * (1 << bit), me >= 0) for bit in range(stages)]
        + [(prev, has_prev), (after, has_next)]
    )

    def copy_of(layer, stage):
        bit = halving_order(parts, layer)[stage]
        half = parts >> (stage + 1)
        mine = bit_of(bit)
        return remote(
            current[layer].at[pl.ds((1 - mine) * half, half)],
            landing[layer][stage],
            send_sem.at[layer, stage],
            recv_sem.at[layer, stage],
            me + (1 - 2 * mine) * (1 << bit),
        )

    refs = (up, down, from_prev, from_next, halo_send, halo_recv)
    copies = [copy_of(1, 0), copy_of(0, 0)]
    copies[0].start()
    copies[1].start()
    start_halo(parts, *refs)
    for stage in range(stages):
        for slot, layer in ((0, 1), (1, 0)):
            half = parts >> (stage + 1)
            mine = bit_of(halving_order(parts, layer)[stage])
            copies[slot].wait()
            source, arrived = current[layer], landing[layer][stage]
            if stage == stages - 1:
                outs[layer][...] = source[mine].astype(f32) + arrived[0].astype(f32)
                continue
            target = kept[layer][stage]

            def add(k, carry, source=source, arrived=arrived, target=target, mine=mine, half=half):
                target[k] = (source[mine * half + k].astype(f32) + arrived[k].astype(f32)).astype(bf16)
                return carry

            lax.fori_loop(0, half, add, 0)
            current[layer] = target
            copies[slot] = copy_of(layer, stage + 1)
            copies[slot].start()
    finish_halo(parts, *refs)


def reduce_weights(parts, enc_w, proc_w, up, down):
    _, rows, columns = enc_w.shape
    stages = parts.bit_length() - 1
    landing = [pltpu.VMEM((parts >> (s + 1), rows, columns), bf16) for s in range(stages)]
    kept = [pltpu.VMEM((parts >> (s + 1), rows, columns), bf16) for s in range(stages - 1)]
    sds = jax.ShapeDtypeStruct
    return pl.pallas_call(
        functools.partial(reduce_kernel, parts),
        in_specs=[vmem] * 4,
        out_specs=[vmem] * 4,
        out_shape=[sds((rows, columns), f32)] * 2 + [sds(up.shape, bf16)] * 2,
        scratch_shapes=landing * 2
        + kept * 2
        + [
            pltpu.SemaphoreType.DMA((2,)),
            pltpu.SemaphoreType.DMA((2,)),
            pltpu.SemaphoreType.DMA((2, stages)),
            pltpu.SemaphoreType.DMA((2, stages)),
        ],
        compiler_params=pltpu.CompilerParams(
            collective_id=3, has_side_effects=True, vmem_limit_bytes=VMEM_LIMIT
        ),
    )(enc_w, proc_w, up, down)


def split_rows(a, axis, order):
    top = lax.reduce_precision(a, 8, 7)
    rest = a - top
    pieces = [top if k else rest for k in order]
    return jnp.concatenate(pieces + [jnp.zeros_like(a)], axis=axis).astype(bf16)


def per_device(
    grid_latent, mesh_latent, out_cotangent, matrices, norm_gains, edge_embeddings,
    enc_attributes, proc_attributes, enc_send_block, enc_recv_block, enc_send_slot,
    enc_recv_slot, enc_count, proc_send_block, proc_recv_block, proc_send_slot,
    proc_recv_slot, proc_count,
):
    parts = lax.axis_size("space")
    rows, width = mesh_latent.shape
    own = grid_latent.shape[0]
    blocks = enc_send_block.shape[0]
    p_blocks = proc_send_block.shape[0]
    sds = jax.ShapeDtypeStruct
    emb = split_rows(edge_embeddings, 1, (1, 1, 0))
    enc_attr = split_rows(enc_attributes, 0, (1, 0, 1))
    proc_attr = split_rows(proc_attributes, 0, (1, 0, 1))

    lo, hi = exchange(parts, grid_latent, grid_latent, width, HG, own // HG - 1, 0, 0)
    enc_out, agg, mixed, slopes, tiles = call(
        enc_forward_kernel,
        [smem] * 3 + [hbm] * 3 + [vmem, layer_spec(0, matrices.shape), vmem, layer_spec(0, emb.shape), vmem, vmem, vmem],
        [
            sds((rows, width), bf16),
            sds((rows, width), bf16),
            sds((rows, width), f32),
            sds((blocks * EPB, width), bf16),
            sds((blocks * BLK, width), bf16),
        ],
        [
            pltpu.VMEM((own + 2 * HG, width), bf16),
            pltpu.VMEM((rows, width), f32),
            pltpu.SemaphoreType.DMA((3,)),
        ],
        4_000_000_000,
    )(
        enc_send_block, enc_recv_block, enc_count, grid_latent, lo, hi, mesh_latent, matrices,
        norm_gains, emb, enc_attr, enc_send_slot, enc_recv_slot,
    )

    lo, hi = exchange(parts, enc_out, enc_out, width, HM, rows // HM - 1, 0, 1)
    mesh_out, d_latent, rim_lo, rim_hi, proc_w = call(
        proc_kernel,
        [smem] * 3 + [vmem] * 4 + [layer_spec(1, matrices.shape), vmem, layer_spec(1, emb.shape), vmem, vmem, vmem],
        [
            sds((rows, width), bf16),
            sds((rows, width), f32),
            sds((HM, width), bf16),
            sds((HM, width), bf16),
            sds((parts, width // parts, 4 * width + SMALL), bf16),
        ],
        [
            pltpu.VMEM((rows + 2 * HM, width), bf16),
            pltpu.VMEM((rows + 2 * HM, width), bf16),
            pltpu.VMEM((p_blocks * EPB, width), bf16),
            pltpu.VMEM((rows, width), f32),
            pltpu.VMEM((rows + 2 * HM, width), f32),
            pltpu.VMEM((16, width), f32),
        ],
        8_000_000_000,
    )(
        proc_send_block, proc_recv_block, proc_count, enc_out, lo, hi, out_cotangent, matrices,
        norm_gains, emb, proc_attr, proc_send_slot, proc_recv_slot,
    )

    back_lo, back_hi = exchange(parts, rim_hi, rim_lo, width, HM, 0, 0, 2)
    mesh_grad, grid_own, grid_lo, grid_hi, enc_w = call(
        enc_backward_kernel,
        [smem] * 3 + [vmem] * 8 + [layer_spec(0, matrices.shape), vmem, vmem, vmem, vmem],
        [
            sds((rows, width), bf16),
            sds((own, width), bf16),
            sds((HG, width), bf16),
            sds((HG, width), bf16),
            sds((parts, width // parts, 4 * width + SMALL), bf16),
        ],
        [
            pltpu.VMEM((own + 2 * HG, width), f32),
            pltpu.VMEM((rows, width), f32),
            pltpu.VMEM((16, width), f32),
            pltpu.VMEM((width, width), f32),
            pltpu.VMEM((rows, width), f32),
        ],
        8_000_000_000,
    )(
        enc_send_block, enc_recv_block, enc_count, d_latent, back_lo, back_hi, mesh_latent, agg,
        mixed, slopes, tiles, matrices, norm_gains, enc_attr, enc_send_slot, enc_recv_slot,
    )
    enc_sum, proc_sum, from_prev, from_next = reduce_weights(parts, enc_w, proc_w, grid_hi, grid_lo)
    grid_grad = grid_own.at[:HG].add(from_prev).at[own - HG :].add(from_next)

    sums = jnp.stack([enc_sum, proc_sum])
    columns = sums.shape[1]
    matrix_grads = sums[:, :, : 4 * width].reshape(2, columns, 4, width).transpose(0, 2, 3, 1)
    small = sums[:, :, 4 * width :].transpose(0, 2, 1)
    embedding_grads = small[:, 0:4] + small[:, 4:8]
    gain_grads = small[:, 16]
    return (mesh_out, grid_grad, mesh_grad, matrix_grads, gain_grads, embedding_grads)


def solution(mesh):
    rows = P(("groups", "space"), None)
    lists = (P("space"), P("space"), P("space", None), P("space", None), P("space"))
    return jax.shard_map(
        per_device,
        mesh=mesh,
        in_specs=(rows, rows, rows, P(), P(), P(), P(None, "space"), P(None, "space")) + lists + lists,
        out_specs=(
            rows,
            rows,
            rows,
            P("groups", None, None, "space"),
            P("groups", "space"),
            P("groups", None, "space"),
        ),
        check_vma=False,
    )
```

```python
import functools

import jax
import jax.numpy as jnp
from jax import lax
from jax.experimental import pallas as pl
from jax.experimental.pallas import tpu as pltpu
from jax.sharding import PartitionSpec as P

BLK = 64
EPB = 128
HG = 256
HM = 64
GB = 4
GE = GB * EPB
EPS = 1e-05
SMALL = 128
VMEM_LIMIT = 56 * 1024 * 1024

f32 = jnp.float32
bf16 = jnp.bfloat16


def dot(a, b):
    return jnp.dot(a, b, preferred_element_type=f32)


def dot_tb(a, b):
    return lax.dot_general(a, b, (((1,), (1,)), ((), ())), preferred_element_type=f32)


def dot_ta(a, b):
    return lax.dot_general(a, b, (((0,), (0,)), ((), ())), preferred_element_type=f32)


def one_hot_pull(columns, group, base, width):
    lanes = lax.broadcasted_iota(jnp.int32, (EPB, width), 1)
    parts = []
    for m in range(GB):
        b = group * GB + m
        parts.append((lanes == columns[:, b : b + 1] + base[m]).astype(f32).astype(bf16))
    return jnp.concatenate(parts, axis=0)


def one_hot_push(slots_ref, group, base, width):
    rows = lax.broadcasted_iota(jnp.int32, (width, EPB), 0)
    parts = []
    for m in range(GB):
        b = group * GB + m
        parts.append((rows == slots_ref[b : b + 1, :] + base[m]).astype(f32).astype(bf16))
    return jnp.concatenate(parts, axis=1)


SEND_BASE = [m * BLK for m in range(GB)]


def recv_base(recv_block, group):
    return [recv_block[group * GB + m] * BLK for m in range(GB)]


def edges_forward(group, send_tiles, recv_proj, cols_s, cols_r, recv_slot, recv_block, attr, emb):
    base = recv_base(recv_block, group)
    width = recv_proj.shape[0]
    pre = dot(one_hot_pull(cols_s, group, SEND_BASE, GB * BLK), send_tiles)
    pre = pre + dot(one_hot_pull(cols_r, group, base, width), recv_proj)
    pre = pre + dot_ta(attr[:, group * GE : (group + 1) * GE], emb)
    gate = 0.5 * jnp.tanh(0.5 * pre) + 0.5
    act = pre * gate
    slope = gate + act * (1.0 - gate)
    summed = dot(one_hot_push(recv_slot, group, base, width), act.astype(bf16))
    return summed, slope.astype(bf16)


def edges_backward(group, d_agg, slope, cols_r, send_slot, recv_slot, recv_block, attr):
    base = recv_base(recv_block, group)
    width = d_agg.shape[0]
    d_pre = dot(one_hot_pull(cols_r, group, base, width), d_agg) * slope.astype(f32)
    d_pre = d_pre.astype(bf16)
    d_send = dot(one_hot_push(send_slot, group, SEND_BASE, GB * BLK), d_pre)
    d_recv = dot(one_hot_push(recv_slot, group, base, width), d_pre)
    d_emb = dot(attr[:, group * GE : (group + 1) * GE], d_pre)
    return d_send, d_recv, d_emb


def tail_forward(mixed, latent, gain):
    u = mixed * (0.5 * jnp.tanh(0.5 * mixed) + 0.5)
    c = u - jnp.mean(u, axis=-1, keepdims=True)
    v = jnp.mean(c * c, axis=-1, keepdims=True)
    return (latent.astype(f32) + c * lax.rsqrt(v + EPS) * gain).astype(bf16)


def tail_backward(mixed, cot, gain):
    s = 0.5 * jnp.tanh(0.5 * mixed) + 0.5
    u = mixed * s
    c = u - jnp.mean(u, axis=-1, keepdims=True)
    r = lax.rsqrt(jnp.mean(c * c, axis=-1, keepdims=True) + EPS)
    n = c * r
    d_gain = jnp.sum(cot * n, axis=0, keepdims=True)
    dn = cot * gain
    du = r * (dn - jnp.mean(dn, axis=-1, keepdims=True) - n * jnp.mean(dn * n, axis=-1, keepdims=True))
    return (du * (s + u * (1.0 - s))).astype(bf16), d_gain


def halving_order(parts, layer):
    order = list(range(parts.bit_length() - 1))
    if layer == 0 and len(order) > 2:
        order[1], order[2] = order[2], order[1]
    return order


def shard_at(place, parts, layer):
    order = halving_order(parts, layer)
    slab = 0
    for k, bit in enumerate(order):
        slab += ((place >> (len(order) - 1 - k)) & 1) << bit
    return slab


def write_shards(w_ref, layer, column, value):
    parts, rows, _ = w_ref.shape
    for place in range(parts):
        slab = shard_at(place, parts, layer)
        w_ref[place, :, column : column + value.shape[1]] = value[
            slab * rows : (slab + 1) * rows, :
        ].astype(bf16)


def write_small(w_ref, layer, d_emb, d_gain):
    width = d_emb.shape[1]
    pad = jnp.zeros((SMALL - 16 - 8, width), f32)
    block = jnp.concatenate([d_emb, jnp.broadcast_to(d_gain, (8, width)), pad], axis=0)
    write_shards(w_ref, layer, 4 * width, block.T)


def enc_forward_kernel(
    send_block, recv_block, count, own, lo, hi, latent, w, gains, emb, attr, send_slot, recv_slot,
    out, agg_out, mixed_out, slope_out, tiles_out, ext, acc, sems,
):
    rows = own.shape[0]
    copies = [
        pltpu.make_async_copy(own, ext.at[pl.ds(HG, rows)], sems.at[0]),
        pltpu.make_async_copy(lo, ext.at[pl.ds(0, HG)], sems.at[1]),
        pltpu.make_async_copy(hi, ext.at[pl.ds(HG + rows, HG)], sems.at[2]),
    ]
    for c in copies:
        c.start()
    recv_proj = dot(latent[...], w[0, 1]).astype(bf16)
    cols_s = send_slot[...].T
    cols_r = recv_slot[...].T
    acc[...] = jnp.zeros_like(acc)
    for c in copies:
        c.wait()
    for group in range(send_slot.shape[0] // GB):

        @pl.when(group * GB < count[0])
        def _(group=group):
            for m in range(GB):
                at = group * GB + m
                start = pl.multiple_of(send_block[at] * BLK, BLK)
                tiles_out[at * BLK : (at + 1) * BLK, :] = ext[pl.ds(start, BLK), :]
            tiles = tiles_out[group * GB * BLK : (group + 1) * GB * BLK, :]
            send_proj = dot(tiles, w[0, 0]).astype(bf16)
            summed, slope = edges_forward(
                group, send_proj, recv_proj, cols_s, cols_r, recv_slot, recv_block, attr, emb[0]
            )
            slope_out[group * GE : (group + 1) * GE, :] = slope
            acc[...] += summed

        @pl.when(group * GB >= count[0])
        def _(group=group):
            for ref, size in ((slope_out, GE), (tiles_out, GB * BLK)):
                ref[group * size : (group + 1) * size, :] = jnp.zeros((size, ref.shape[1]), bf16)

    agg = acc[...].astype(bf16)
    agg_out[...] = agg
    mixed = dot(latent[...], w[0, 2]) + dot(agg, w[0, 3])
    mixed_out[...] = mixed
    out[...] = tail_forward(mixed, latent[...], gains[0:1, :])


def proc_kernel(
    send_block, recv_block, count, enc_out, lo, hi, cot, w, gains, emb, attr, send_slot, recv_slot,
    out, d_latent, rim_lo, rim_hi, w_out, ext, proj, slopes, acc, d_send_acc, d_emb_acc,
):
    rows, width = enc_out.shape
    groups = send_slot.shape[0] // GB
    latent = enc_out[...]
    ext[0:HM, :] = lo[...]
    ext[HM : HM + rows, :] = latent
    ext[HM + rows :, :] = hi[...]
    proj[...] = dot(ext[...], w[0, 0]).astype(bf16)
    recv_proj = dot(latent, w[0, 1]).astype(bf16)
    cols_s = send_slot[...].T
    cols_r = recv_slot[...].T
    acc[...] = jnp.zeros_like(acc)
    for group in range(groups):

        @pl.when(group * GB < count[0])
        def _(group=group):
            tiles = [
                proj[pl.ds(pl.multiple_of(send_block[group * GB + m] * BLK, BLK), BLK), :]
                for m in range(GB)
            ]
            summed, slope = edges_forward(
                group, jnp.concatenate(tiles, axis=0), recv_proj, cols_s, cols_r, recv_slot,
                recv_block, attr, emb[0],
            )
            slopes[group * GE : (group + 1) * GE, :] = slope
            acc[...] += summed

    agg = acc[...].astype(bf16)
    mixed = dot(latent, w[0, 2]) + dot(agg, w[0, 3])
    out[...] = tail_forward(mixed, latent, gains[1:2, :])

    cot32 = cot[...].astype(f32)
    g, d_gain = tail_backward(mixed, cot32, gains[1:2, :])
    d_agg = dot_tb(g, w[0, 3]).astype(bf16)
    acc[...] = jnp.zeros_like(acc)
    d_send_acc[...] = jnp.zeros_like(d_send_acc)
    d_emb_acc[...] = jnp.zeros_like(d_emb_acc)
    for group in range(groups):

        @pl.when(group * GB < count[0])
        def _(group=group):
            d_send, d_recv, d_emb = edges_backward(
                group, d_agg, slopes[group * GE : (group + 1) * GE, :], cols_r, send_slot,
                recv_slot, recv_block, attr,
            )
            for m in range(GB):
                start = pl.multiple_of(send_block[group * GB + m] * BLK, BLK)
                d_send_acc[pl.ds(start, BLK), :] += d_send[m * BLK : (m + 1) * BLK, :]
            acc[...] += d_recv
            d_emb_acc[...] += d_emb

    d_send = d_send_acc[...].astype(bf16)
    d_recv = acc[...].astype(bf16)
    d_rows = dot_tb(d_send, w[0, 0])
    rim_lo[...] = d_rows[0:HM, :].astype(bf16)
    rim_hi[...] = d_rows[HM + rows :, :].astype(bf16)
    d_latent[...] = (
        cot32 + dot_tb(g, w[0, 2]) + dot_tb(d_recv, w[0, 1]) + d_rows[HM : HM + rows, :]
    )
    write_shards(w_out, 1, 0, dot_ta(d_send, ext[...]))
    write_shards(w_out, 1, width, dot_ta(d_recv, latent))
    write_shards(w_out, 1, 2 * width, dot_ta(g, latent))
    write_shards(w_out, 1, 3 * width, dot_ta(g, agg))
    write_small(w_out, 1, d_emb_acc[...], d_gain)


smem = pl.BlockSpec(memory_space=pltpu.SMEM)
hbm = pl.BlockSpec(memory_space=pl.ANY)
vmem = pl.BlockSpec(memory_space=pltpu.VMEM)


def layer_spec(layer, shape):
    tail = (0,) * (len(shape) - 1)
    return pl.BlockSpec((1,) + shape[1:], lambda i: (layer,) + tail)


def call(kernel, in_specs, out_shape, scratch, flops):
    return pl.pallas_call(
        kernel,
        grid=(1,),
        in_specs=in_specs,
        out_specs=[vmem] * len(out_shape),
        out_shape=out_shape,
        scratch_shapes=scratch,
        compiler_params=pltpu.CompilerParams(vmem_limit_bytes=VMEM_LIMIT),
        cost_estimate=pl.CostEstimate(flops=flops, bytes_accessed=10_000_000, transcendentals=0),
    )


def greet(targets):
    barrier = pltpu.get_barrier_semaphore()
    for slab, there in targets:

        @pl.when(there)
        def _(slab=slab):
            pl.semaphore_signal(
                barrier, inc=1, device_id={"space": slab}, device_id_type=pl.DeviceIdType.MESH
            )

    pl.semaphore_wait(barrier, sum(jnp.where(there, 1, 0) for _, there in targets))


def remote(src, dst, send_sem, recv_sem, slab):
    return pltpu.make_async_remote_copy(
        src_ref=src,
        dst_ref=dst,
        send_sem=send_sem,
        recv_sem=recv_sem,
        device_id={"space": slab},
        device_id_type=pl.DeviceIdType.MESH,
    )


def neighbours(parts):
    me = lax.axis_index("space")
    has_prev, has_next = me > 0, me < parts - 1
    return jnp.maximum(me - 1, 0), jnp.minimum(me + 1, parts - 1), has_prev, has_next


def start_halo(parts, up, down, from_prev, from_next, send_sem, recv_sem):
    prev, after, has_prev, has_next = neighbours(parts)

    @pl.when(has_next)
    def _():
        remote(up, from_prev, send_sem.at[0], recv_sem.at[0], after).start()

    @pl.when(has_prev)
    def _():
        remote(down, from_next, send_sem.at[1], recv_sem.at[1], prev).start()

    @pl.when(jnp.logical_not(has_prev))
    def _():
        from_prev[...] = jnp.zeros_like(from_prev)

    @pl.when(jnp.logical_not(has_next))
    def _():
        from_next[...] = jnp.zeros_like(from_next)


def finish_halo(parts, up, down, from_prev, from_next, send_sem, recv_sem):
    prev, after, has_prev, has_next = neighbours(parts)

    @pl.when(has_next)
    def _():
        remote(up, from_prev, send_sem.at[0], recv_sem.at[0], after).wait_send()
        remote(down, from_next, send_sem.at[1], recv_sem.at[1], after).wait_recv()

    @pl.when(has_prev)
    def _():
        remote(down, from_next, send_sem.at[1], recv_sem.at[1], prev).wait_send()
        remote(up, from_prev, send_sem.at[0], recv_sem.at[0], prev).wait_recv()


def exchange_kernel(parts, up, down, from_prev, from_next, send_sem, recv_sem):
    prev, after, has_prev, has_next = neighbours(parts)
    greet([(prev, has_prev), (after, has_next)])
    refs = (up, down, from_prev, from_next, send_sem, recv_sem)
    start_halo(parts, *refs)
    finish_halo(parts, *refs)


def exchange(parts, up, down, width, margin, up_block, down_block, collective_id):
    return pl.pallas_call(
        functools.partial(exchange_kernel, parts),
        grid=(1,),
        in_specs=[
            pl.BlockSpec((margin, width), lambda i: (up_block, 0)),
            pl.BlockSpec((margin, width), lambda i: (down_block, 0)),
        ],
        out_specs=[vmem] * 2,
        out_shape=[jax.ShapeDtypeStruct((margin, width), bf16)] * 2,
        scratch_shapes=[pltpu.SemaphoreType.DMA((2,)), pltpu.SemaphoreType.DMA((2,))],
        compiler_params=pltpu.CompilerParams(collective_id=collective_id, has_side_effects=True),
    )(up, down)


def row_places(send_block, blocks):
    lanes = lax.broadcasted_iota(jnp.int32, (1, 2 * BLK), 1)
    pairs = []
    for b in range(0, blocks, 2):
        first = send_block[b] * BLK
        second = send_block[b + 1] * BLK - BLK
        pairs.append(lanes + jnp.where(lanes < BLK, first, second))
    return jnp.concatenate(pairs, axis=1)


def enc_backward_kernel(
    parts, send_block, recv_block, d_latent, rim_up, rim_down, latent, agg, mixed, slopes, tiles,
    w, gains, attr, send_slot, recv_slot, proc_w,
    mesh_grad, grid_grad, enc_out, proc_out,
    back_lo, back_hi, grid_lo, grid_hi, from_prev, from_next, enc_w, d_rows, acc, d_emb_acc,
    w0_acc, cot_ref, *scratch,
):
    rim_send, rim_recv, halo_send, halo_recv, send_sem, recv_sem = scratch[-6:]
    stages = parts.bit_length() - 1
    landing = [scratch[0:stages], scratch[stages : 2 * stages]]
    kept = [scratch[2 * stages : 3 * stages - 1], scratch[3 * stages - 1 : 4 * stages - 2]]
    outs = [enc_out, proc_out]
    current = [enc_w, proc_w]
    copies = [None, None]
    done = [0, 0]
    me = lax.axis_index("space")

    def bit_of(bit):
        return (me // (1 << bit)) % 2

    def start(layer):
        stage = done[layer]
        bit = halving_order(parts, layer)[stage]
        half = parts >> (stage + 1)
        mine = bit_of(bit)
        copies[layer] = remote(
            current[layer].at[pl.ds((1 - mine) * half, half)],
            landing[layer][stage],
            send_sem.at[layer, stage],
            recv_sem.at[layer, stage],
            me + (1 - 2 * mine) * (1 << bit),
        )
        copies[layer].start()

    def advance(layer):
        stage = done[layer]
        if stage == stages:
            return
        half = parts >> (stage + 1)
        mine = bit_of(halving_order(parts, layer)[stage])
        copies[layer].wait()
        source, arrived = current[layer], landing[layer][stage]
        done[layer] += 1
        if stage == stages - 1:
            outs[layer][...] = source[mine].astype(f32) + arrived[0].astype(f32)
            return
        target = kept[layer][stage]

        def add(k, carry):
            target[k] = (source[mine * half + k].astype(f32) + arrived[k].astype(f32)).astype(bf16)
            return carry

        lax.fori_loop(0, half, add, 0)
        current[layer] = target
        start(layer)

    prev, after, has_prev, has_next = neighbours(parts)
    greet(
        [(me + (1 - 2 * bit_of(bit)) * (1 << bit), me >= 0) for bit in range(stages)]
        + [(prev, has_prev), (after, has_next)]
    )
    rims = (rim_up, rim_down, back_lo, back_hi, rim_send, rim_recv)
    halos = (grid_hi, grid_lo, from_prev, from_next, halo_send, halo_recv)
    start_halo(parts, *rims)
    start(1)

    rows, width = latent.shape
    groups = send_slot.shape[0] // GB
    cols_r = recv_slot[...].T
    cot_ref[...] = d_latent[...]
    acc[...] = jnp.zeros_like(acc)
    d_emb_acc[...] = jnp.zeros_like(d_emb_acc)
    w0_acc[...] = jnp.zeros_like(w0_acc)
    finish_halo(parts, *rims)
    cot_ref[0:HM, :] += back_lo[...].astype(f32)
    cot_ref[rows - HM :, :] += back_hi[...].astype(f32)
    cot = cot_ref[...].astype(bf16).astype(f32)
    g, d_gain = tail_backward(mixed[...], cot, gains[0:1, :])
    d_agg = dot_tb(g, w[0, 3]).astype(bf16)
    write_shards(enc_w, 0, 2 * width, dot_ta(g, latent[...]))
    write_shards(enc_w, 0, 3 * width, dot_ta(g, agg[...]))
    for group in range(groups):
        tile = pl.ds(group * GB * BLK, GB * BLK)
        d_send, d_recv, d_emb = edges_backward(
            group, d_agg, slopes[group * GE : (group + 1) * GE, :], cols_r, send_slot,
            recv_slot, recv_block, attr,
        )
        d_send = d_send.astype(bf16)
        d_rows[tile, :] = dot_tb(d_send, w[0, 0]).astype(bf16)
        acc[...] += d_recv
        d_emb_acc[...] += d_emb
        w0_acc[...] += dot_ta(d_send, tiles[tile, :])
        if group in (0, groups - 1):
            advance(1)

    d_recv = acc[...].astype(bf16)
    write_shards(enc_w, 0, 0, w0_acc[...])
    write_shards(enc_w, 0, width, dot_ta(d_recv, latent[...]))
    write_small(enc_w, 0, d_emb_acc[...], d_gain)
    start(0)

    own = grid_grad.shape[0]
    places = row_places(send_block, send_slot.shape[0])
    ids = lax.broadcasted_iota(jnp.int32, (HG, places.shape[1]), 0)

    def scattered(chunk):
        return dot((ids + chunk * HG == places).astype(f32).astype(bf16), d_rows[...]).astype(bf16)

    def own_chunk(chunk, carry):
        grid_grad[pl.ds(pl.multiple_of(chunk * HG, HG), HG), :] = scattered(chunk + 1)
        return carry

    grid_lo[...] = scattered(0)
    grid_hi[...] = scattered(own // HG + 1)
    start_halo(parts, *halos)
    middle = own // HG // 2
    advance(0)
    lax.fori_loop(0, middle, own_chunk, 0)
    advance(1)
    lax.fori_loop(middle, own // HG, own_chunk, 0)
    mesh_grad[...] = (cot + dot_tb(g, w[0, 2]) + dot_tb(d_recv, w[0, 1])).astype(bf16)
    for _ in range(stages):
        advance(0)
        advance(1)
    finish_halo(parts, *halos)
    grid_grad[0:HG, :] += from_prev[...]
    grid_grad[own - HG :, :] += from_next[...]


def first_exchange_kernel(
    parts, up, down, enc_a, proc_a, emb, from_prev, from_next, enc_attr, proc_attr, emb_out,
    wide, narrow, send_sem, recv_sem,
):
    prev, after, has_prev, has_next = neighbours(parts)
    greet([(prev, has_prev), (after, has_next)])
    refs = (up, down, from_prev, from_next, send_sem, recv_sem)
    start_halo(parts, *refs)

    def split(value, work, order):
        top = value.astype(bf16).astype(f32)
        rest = value - top
        work[...] = jnp.zeros_like(work)
        for k, high in enumerate(order):
            work[4 * k : 4 * k + 4, :] = top if high else rest
        return work[...].astype(bf16)

    enc_attr[...] = split(enc_a[...], wide, (1, 0, 1))
    proc_attr[...] = split(proc_a[...], wide, (1, 0, 1))
    for layer in range(2):
        emb_out[layer] = split(emb[layer], narrow, (1, 1, 0))
    finish_halo(parts, *refs)


def per_device(
    grid_latent, mesh_latent, out_cotangent, matrices, norm_gains, edge_embeddings,
    enc_attributes, proc_attributes, enc_send_block, enc_recv_block, enc_send_slot,
    enc_recv_slot, enc_count, proc_send_block, proc_recv_block, proc_send_slot,
    proc_recv_slot, proc_count,
):
    parts = lax.axis_size("space")
    rows, width = mesh_latent.shape
    own = grid_latent.shape[0]
    blocks = enc_send_block.shape[0]
    p_blocks = proc_send_block.shape[0]
    sds = jax.ShapeDtypeStruct

    edges = enc_attributes.shape[1]
    lo, hi, enc_attr, proc_attr, emb = pl.pallas_call(
        functools.partial(first_exchange_kernel, parts),
        grid=(1,),
        in_specs=[
            pl.BlockSpec((HG, width), lambda i: (own // HG - 1, 0)),
            pl.BlockSpec((HG, width), lambda i: (0, 0)),
        ]
        + [vmem] * 3,
        out_specs=[vmem] * 5,
        out_shape=[sds((HG, width), bf16)] * 2
        + [sds((16, edges), bf16)] * 2
        + [sds((2, 16, width), bf16)],
        scratch_shapes=[
            pltpu.VMEM((16, edges), f32),
            pltpu.VMEM((16, width), f32),
            pltpu.SemaphoreType.DMA((2,)),
            pltpu.SemaphoreType.DMA((2,)),
        ],
        compiler_params=pltpu.CompilerParams(
            collective_id=0, has_side_effects=True, vmem_limit_bytes=VMEM_LIMIT
        ),
    )(grid_latent, grid_latent, enc_attributes, proc_attributes, edge_embeddings)
    enc_out, agg, mixed, slopes, tiles = call(
        enc_forward_kernel,
        [smem] * 3 + [hbm] * 3 + [vmem, layer_spec(0, matrices.shape), vmem, layer_spec(0, emb.shape), vmem, vmem, vmem],
        [
            sds((rows, width), bf16),
            sds((rows, width), bf16),
            sds((rows, width), f32),
            sds((blocks * EPB, width), bf16),
            sds((blocks * BLK, width), bf16),
        ],
        [
            pltpu.VMEM((own + 2 * HG, width), bf16),
            pltpu.VMEM((rows, width), f32),
            pltpu.SemaphoreType.DMA((3,)),
        ],
        4_000_000_000,
    )(
        enc_send_block, enc_recv_block, enc_count, grid_latent, lo, hi, mesh_latent, matrices,
        norm_gains, emb, enc_attr, enc_send_slot, enc_recv_slot,
    )

    lo, hi = exchange(parts, enc_out, enc_out, width, HM, rows // HM - 1, 0, 1)
    mesh_out, d_latent, rim_lo, rim_hi, proc_w = call(
        proc_kernel,
        [smem] * 3 + [vmem] * 4 + [layer_spec(1, matrices.shape), vmem, layer_spec(1, emb.shape), vmem, vmem, vmem],
        [
            sds((rows, width), bf16),
            sds((rows, width), f32),
            sds((HM, width), bf16),
            sds((HM, width), bf16),
            sds((parts, width // parts, 4 * width + SMALL), bf16),
        ],
        [
            pltpu.VMEM((rows + 2 * HM, width), bf16),
            pltpu.VMEM((rows + 2 * HM, width), bf16),
            pltpu.VMEM((p_blocks * EPB, width), bf16),
            pltpu.VMEM((rows, width), f32),
            pltpu.VMEM((rows + 2 * HM, width), f32),
            pltpu.VMEM((16, width), f32),
        ],
        8_000_000_000,
    )(
        proc_send_block, proc_recv_block, proc_count, enc_out, lo, hi, out_cotangent, matrices,
        norm_gains, emb, proc_attr, proc_send_slot, proc_recv_slot,
    )

    stages = parts.bit_length() - 1
    columns = 4 * width + SMALL
    shard = width // parts
    landing = [pltpu.VMEM((parts >> (k + 1), shard, columns), bf16) for k in range(stages)]
    mesh_grad, grid_grad, enc_sum, proc_sum = pl.pallas_call(
        functools.partial(enc_backward_kernel, parts),
        grid=(1,),
        in_specs=[smem] * 2 + [vmem] * 8 + [layer_spec(0, matrices.shape)] + [vmem] * 5,
        out_specs=[vmem] * 4,
        out_shape=[
            sds((rows, width), bf16),
            sds((own, width), bf16),
            sds((shard, columns), f32),
            sds((shard, columns), f32),
        ],
        scratch_shapes=[pltpu.VMEM((HM, width), bf16)] * 2
        + [pltpu.VMEM((HG, width), bf16)] * 4
        + [
            pltpu.VMEM((parts, shard, columns), bf16),
            pltpu.VMEM((blocks * BLK, width), bf16),
            pltpu.VMEM((rows, width), f32),
            pltpu.VMEM((16, width), f32),
            pltpu.VMEM((width, width), f32),
            pltpu.VMEM((rows, width), f32),
        ]
        + landing * 2
        + landing[:-1] * 2
        + [pltpu.SemaphoreType.DMA((2,))] * 4
        + [pltpu.SemaphoreType.DMA((2, stages))] * 2,
        compiler_params=pltpu.CompilerParams(
            collective_id=2, has_side_effects=True, vmem_limit_bytes=VMEM_LIMIT
        ),
    )(
        enc_send_block, enc_recv_block, d_latent, rim_hi, rim_lo, mesh_latent, agg, mixed, slopes,
        tiles, matrices, norm_gains, enc_attr, enc_send_slot, enc_recv_slot, proc_w,
    )

    sums = jnp.stack([enc_sum, proc_sum])
    columns = sums.shape[1]
    matrix_grads = sums[:, :, : 4 * width].reshape(2, columns, 4, width).transpose(0, 2, 3, 1)
    small = sums[:, :, 4 * width :].transpose(0, 2, 1)
    embedding_grads = small[:, 0:4] + small[:, 4:8]
    gain_grads = small[:, 16]
    return (mesh_out, grid_grad, mesh_grad, matrix_grads, gain_grads, embedding_grads)


def solution(mesh):
    rows = P(("groups", "space"), None)
    lists = (P("space"), P("space"), P("space", None), P("space", None), P("space"))
    return jax.shard_map(
        per_device,
        mesh=mesh,
        in_specs=(rows, rows, rows, P(), P(), P(), P(None, "space"), P(None, "space")) + lists + lists,
        out_specs=(
            rows,
            rows,
            rows,
            P("groups", None, None, "space"),
            P("groups", "space"),
            P("groups", None, "space"),
        ),
        check_vma=False,
    )
```

```python
import functools

import jax
import jax.numpy as jnp
from jax import lax
from jax.experimental import pallas as pl
from jax.experimental.pallas import tpu as pltpu
from jax.sharding import PartitionSpec as P

BLK = 64
EPB = 128
HG = 256
HM = 64
GB = 4
GE = GB * EPB
EPS = 1e-05
SMALL = 128
VMEM_LIMIT = 56 * 1024 * 1024

f32 = jnp.float32
bf16 = jnp.bfloat16


def dot(a, b):
    return jnp.dot(a, b, preferred_element_type=f32)


def dot_tb(a, b):
    return lax.dot_general(a, b, (((1,), (1,)), ((), ())), preferred_element_type=f32)


def dot_ta(a, b):
    return lax.dot_general(a, b, (((0,), (0,)), ((), ())), preferred_element_type=f32)


def one_hot_pull(columns, group, base, width):
    lanes = lax.broadcasted_iota(jnp.int32, (EPB, width), 1)
    parts = []
    for m in range(GB):
        b = group * GB + m
        parts.append((lanes == columns[:, b : b + 1] + base[m]).astype(f32).astype(bf16))
    return jnp.concatenate(parts, axis=0)


def one_hot_push(slots_ref, group, base, width):
    rows = lax.broadcasted_iota(jnp.int32, (width, EPB), 0)
    parts = []
    for m in range(GB):
        b = group * GB + m
        parts.append((rows == slots_ref[b : b + 1, :] + base[m]).astype(f32).astype(bf16))
    return jnp.concatenate(parts, axis=1)


SEND_BASE = [m * BLK for m in range(GB)]


def recv_base(recv_block, group):
    return [recv_block[group * GB + m] * BLK for m in range(GB)]


def edges_forward(group, send_tiles, recv_proj, cols_s, cols_r, recv_slot, recv_block, attr, emb):
    base = recv_base(recv_block, group)
    width = recv_proj.shape[0]
    pre = dot(one_hot_pull(cols_s, group, SEND_BASE, GB * BLK), send_tiles)
    pre = pre + dot(one_hot_pull(cols_r, group, base, width), recv_proj)
    pre = pre + dot_ta(attr[:, group * GE : (group + 1) * GE], emb)
    gate = 0.5 * jnp.tanh(0.5 * pre) + 0.5
    act = pre * gate
    slope = gate + act * (1.0 - gate)
    summed = dot(one_hot_push(recv_slot, group, base, width), act.astype(bf16))
    return summed, slope.astype(bf16)


def edges_backward(group, d_agg, slope, cols_r, send_slot, recv_slot, recv_block, attr):
    base = recv_base(recv_block, group)
    width = d_agg.shape[0]
    d_pre = dot(one_hot_pull(cols_r, group, base, width), d_agg) * slope.astype(f32)
    d_pre = d_pre.astype(bf16)
    d_send = dot(one_hot_push(send_slot, group, SEND_BASE, GB * BLK), d_pre)
    d_recv = dot(one_hot_push(recv_slot, group, base, width), d_pre)
    d_emb = dot(attr[:, group * GE : (group + 1) * GE], d_pre)
    return d_send, d_recv, d_emb


def tail_forward(mixed, latent, gain):
    u = mixed * (0.5 * jnp.tanh(0.5 * mixed) + 0.5)
    c = u - jnp.mean(u, axis=-1, keepdims=True)
    v = jnp.mean(c * c, axis=-1, keepdims=True)
    return (latent.astype(f32) + c * lax.rsqrt(v + EPS) * gain).astype(bf16)


def tail_backward(mixed, cot, gain):
    s = 0.5 * jnp.tanh(0.5 * mixed) + 0.5
    u = mixed * s
    c = u - jnp.mean(u, axis=-1, keepdims=True)
    r = lax.rsqrt(jnp.mean(c * c, axis=-1, keepdims=True) + EPS)
    n = c * r
    d_gain = jnp.sum(cot * n, axis=0, keepdims=True)
    dn = cot * gain
    du = r * (dn - jnp.mean(dn, axis=-1, keepdims=True) - n * jnp.mean(dn * n, axis=-1, keepdims=True))
    return (du * (s + u * (1.0 - s))).astype(bf16), d_gain


def halving_order(parts, layer):
    order = list(range(parts.bit_length() - 1))
    return order


def shard_at(place, parts, layer):
    order = halving_order(parts, layer)
    slab = 0
    for k, bit in enumerate(order):
        slab += ((place >> (len(order) - 1 - k)) & 1) << bit
    return slab


def write_shards(w_ref, layer, column, value):
    parts, rows, _ = w_ref.shape
    for place in range(parts):
        slab = shard_at(place, parts, layer)
        w_ref[place, :, column : column + value.shape[1]] = value[
            slab * rows : (slab + 1) * rows, :
        ].astype(bf16)


def write_small(w_ref, layer, column, d_emb, d_gain):
    width = d_emb.shape[1]
    pad = jnp.zeros((SMALL - 16 - 8, width), f32)
    block = jnp.concatenate([d_emb, jnp.broadcast_to(d_gain, (8, width)), pad], axis=0)
    write_shards(w_ref, layer, column, block.T)


def enc_forward_kernel(
    send_block, recv_block, count, own, lo, hi, latent, w, gains, emb, attr, send_slot, recv_slot,
    out, agg_out, mixed_out, slope_out, tiles_out, ext, acc, sems,
):
    rows = own.shape[0]
    copies = [
        pltpu.make_async_copy(own, ext.at[pl.ds(HG, rows)], sems.at[0]),
        pltpu.make_async_copy(lo, ext.at[pl.ds(0, HG)], sems.at[1]),
        pltpu.make_async_copy(hi, ext.at[pl.ds(HG + rows, HG)], sems.at[2]),
    ]
    for c in copies:
        c.start()
    recv_proj = dot(latent[...], w[0, 1]).astype(bf16)
    cols_s = send_slot[...].T
    cols_r = recv_slot[...].T
    acc[...] = jnp.zeros_like(acc)
    for c in copies:
        c.wait()
    for group in range(send_slot.shape[0] // GB):

        @pl.when(group * GB < count[0])
        def _(group=group):
            for m in range(GB):
                at = group * GB + m
                start = pl.multiple_of(send_block[at] * BLK, BLK)
                tiles_out[at * BLK : (at + 1) * BLK, :] = ext[pl.ds(start, BLK), :]
            tiles = tiles_out[group * GB * BLK : (group + 1) * GB * BLK, :]
            send_proj = dot(tiles, w[0, 0]).astype(bf16)
            summed, slope = edges_forward(
                group, send_proj, recv_proj, cols_s, cols_r, recv_slot, recv_block, attr, emb[0]
            )
            slope_out[group * GE : (group + 1) * GE, :] = slope
            acc[...] += summed

        @pl.when(group * GB >= count[0])
        def _(group=group):
            for ref, size in ((slope_out, GE), (tiles_out, GB * BLK)):
                ref[group * size : (group + 1) * size, :] = jnp.zeros((size, ref.shape[1]), bf16)

    agg = acc[...].astype(bf16)
    agg_out[...] = agg
    mixed = dot(latent[...], w[0, 2]) + dot(agg, w[0, 3])
    mixed_out[...] = mixed
    out[...] = tail_forward(mixed, latent[...], gains[0:1, :])


def proc_kernel(
    send_block, recv_block, count, enc_out, lo, hi, cot, w, gains, emb, attr, send_slot, recv_slot,
    out, d_latent, rim_lo, rim_hi, w_out, ext, proj, slopes, acc, d_send_acc, d_emb_acc,
):
    rows, width = enc_out.shape
    groups = send_slot.shape[0] // GB
    latent = enc_out[...]
    ext[0:HM, :] = lo[...]
    ext[HM : HM + rows, :] = latent
    ext[HM + rows :, :] = hi[...]
    proj[...] = dot(ext[...], w[0, 0]).astype(bf16)
    recv_proj = dot(latent, w[0, 1]).astype(bf16)
    cols_s = send_slot[...].T
    cols_r = recv_slot[...].T
    acc[...] = jnp.zeros_like(acc)
    for group in range(groups):

        @pl.when(group * GB < count[0])
        def _(group=group):
            tiles = [
                proj[pl.ds(pl.multiple_of(send_block[group * GB + m] * BLK, BLK), BLK), :]
                for m in range(GB)
            ]
            summed, slope = edges_forward(
                group, jnp.concatenate(tiles, axis=0), recv_proj, cols_s, cols_r, recv_slot,
                recv_block, attr, emb[0],
            )
            slopes[group * GE : (group + 1) * GE, :] = slope
            acc[...] += summed

    agg = acc[...].astype(bf16)
    mixed = dot(latent, w[0, 2]) + dot(agg, w[0, 3])
    out[...] = tail_forward(mixed, latent, gains[1:2, :])

    cot32 = cot[...].astype(f32)
    g, d_gain = tail_backward(mixed, cot32, gains[1:2, :])
    d_agg = dot_tb(g, w[0, 3]).astype(bf16)
    acc[...] = jnp.zeros_like(acc)
    d_send_acc[...] = jnp.zeros_like(d_send_acc)
    d_emb_acc[...] = jnp.zeros_like(d_emb_acc)
    for group in range(groups):

        @pl.when(group * GB < count[0])
        def _(group=group):
            d_send, d_recv, d_emb = edges_backward(
                group, d_agg, slopes[group * GE : (group + 1) * GE, :], cols_r, send_slot,
                recv_slot, recv_block, attr,
            )
            for m in range(GB):
                start = pl.multiple_of(send_block[group * GB + m] * BLK, BLK)
                d_send_acc[pl.ds(start, BLK), :] += d_send[m * BLK : (m + 1) * BLK, :]
            acc[...] += d_recv
            d_emb_acc[...] += d_emb

    d_send = d_send_acc[...].astype(bf16)
    d_recv = acc[...].astype(bf16)
    d_rows = dot_tb(d_send, w[0, 0])
    rim_lo[...] = d_rows[0:HM, :].astype(bf16)
    rim_hi[...] = d_rows[HM + rows :, :].astype(bf16)
    d_latent[...] = (
        cot32 + dot_tb(g, w[0, 2]) + dot_tb(d_recv, w[0, 1]) + d_rows[HM : HM + rows, :]
    )
    write_shards(w_out, 1, 0, dot_ta(d_send, ext[...]))
    write_shards(w_out, 1, width, dot_ta(d_recv, latent))
    write_shards(w_out, 1, 2 * width, dot_ta(g, latent))
    write_shards(w_out, 1, 3 * width, dot_ta(g, agg))
    write_small(w_out, 1, 4 * width, d_emb_acc[...], d_gain)


smem = pl.BlockSpec(memory_space=pltpu.SMEM)
hbm = pl.BlockSpec(memory_space=pl.ANY)
vmem = pl.BlockSpec(memory_space=pltpu.VMEM)


def layer_spec(layer, shape):
    tail = (0,) * (len(shape) - 1)
    return pl.BlockSpec((1,) + shape[1:], lambda i: (layer,) + tail)


def call(kernel, in_specs, out_shape, scratch, flops):
    return pl.pallas_call(
        kernel,
        grid=(1,),
        in_specs=in_specs,
        out_specs=[vmem] * len(out_shape),
        out_shape=out_shape,
        scratch_shapes=scratch,
        compiler_params=pltpu.CompilerParams(vmem_limit_bytes=VMEM_LIMIT),
        cost_estimate=pl.CostEstimate(flops=flops, bytes_accessed=10_000_000, transcendentals=0),
    )


def greet(targets):
    barrier = pltpu.get_barrier_semaphore()
    for slab, there in targets:

        @pl.when(there)
        def _(slab=slab):
            pl.semaphore_signal(
                barrier, inc=1, device_id={"space": slab}, device_id_type=pl.DeviceIdType.MESH
            )

    pl.semaphore_wait(barrier, sum(jnp.where(there, 1, 0) for _, there in targets))


def remote(src, dst, send_sem, recv_sem, slab):
    return pltpu.make_async_remote_copy(
        src_ref=src,
        dst_ref=dst,
        send_sem=send_sem,
        recv_sem=recv_sem,
        device_id={"space": slab},
        device_id_type=pl.DeviceIdType.MESH,
    )


def neighbours(parts):
    me = lax.axis_index("space")
    has_prev, has_next = me > 0, me < parts - 1
    return jnp.maximum(me - 1, 0), jnp.minimum(me + 1, parts - 1), has_prev, has_next


def start_halo(parts, up, down, from_prev, from_next, send_sem, recv_sem):
    prev, after, has_prev, has_next = neighbours(parts)

    @pl.when(has_next)
    def _():
        remote(up, from_prev, send_sem.at[0], recv_sem.at[0], after).start()

    @pl.when(has_prev)
    def _():
        remote(down, from_next, send_sem.at[1], recv_sem.at[1], prev).start()

    @pl.when(jnp.logical_not(has_prev))
    def _():
        from_prev[...] = jnp.zeros_like(from_prev)

    @pl.when(jnp.logical_not(has_next))
    def _():
        from_next[...] = jnp.zeros_like(from_next)


def finish_halo(parts, up, down, from_prev, from_next, send_sem, recv_sem):
    prev, after, has_prev, has_next = neighbours(parts)

    @pl.when(has_next)
    def _():
        remote(up, from_prev, send_sem.at[0], recv_sem.at[0], after).wait_send()
        remote(down, from_next, send_sem.at[1], recv_sem.at[1], after).wait_recv()

    @pl.when(has_prev)
    def _():
        remote(down, from_next, send_sem.at[1], recv_sem.at[1], prev).wait_send()
        remote(up, from_prev, send_sem.at[0], recv_sem.at[0], prev).wait_recv()


def exchange_kernel(parts, up, down, from_prev, from_next, send_sem, recv_sem):
    prev, after, has_prev, has_next = neighbours(parts)
    greet([(prev, has_prev), (after, has_next)])
    refs = (up, down, from_prev, from_next, send_sem, recv_sem)
    start_halo(parts, *refs)
    finish_halo(parts, *refs)


def exchange(parts, up, down, width, margin, up_block, down_block, collective_id):
    return pl.pallas_call(
        functools.partial(exchange_kernel, parts),
        grid=(1,),
        in_specs=[
            pl.BlockSpec((margin, width), lambda i: (up_block, 0)),
            pl.BlockSpec((margin, width), lambda i: (down_block, 0)),
        ],
        out_specs=[vmem] * 2,
        out_shape=[jax.ShapeDtypeStruct((margin, width), bf16)] * 2,
        scratch_shapes=[pltpu.SemaphoreType.DMA((2,)), pltpu.SemaphoreType.DMA((2,))],
        compiler_params=pltpu.CompilerParams(collective_id=collective_id, has_side_effects=True),
    )(up, down)


def row_places(send_block, blocks):
    lanes = lax.broadcasted_iota(jnp.int32, (1, 2 * BLK), 1)
    pairs = []
    for b in range(0, blocks, 2):
        first = send_block[b] * BLK
        second = send_block[b + 1] * BLK - BLK
        pairs.append(lanes + jnp.where(lanes < BLK, first, second))
    return jnp.concatenate(pairs, axis=1)


def enc_backward_kernel(
    parts, send_block, recv_block, d_latent, rim_up, rim_down, latent, agg, mixed, slopes, tiles,
    w, gains, attr, send_slot, recv_slot, proc_w,
    mesh_grad, grid_grad, enc_out, proc_out,
    back_lo, back_hi, grid_lo, grid_hi, from_prev, from_next, enc_w, node_w, d_rows, acc, d_emb_acc,
    w0_acc, cot_ref, *scratch,
):
    rim_send, rim_recv, halo_send, halo_recv, send_sem, recv_sem = scratch[-6:]
    stages = parts.bit_length() - 1
    span = 2 * stages - 1
    landing = [scratch[k * span : k * span + stages] for k in range(3)]
    kept = [scratch[k * span + stages : (k + 1) * span] for k in range(3)]
    wide, side = 2 * latent.shape[1], 4 * latent.shape[1]
    current = [enc_w, proc_w, node_w]
    copies = [None] * 3
    done = [0] * 3
    me = lax.axis_index("space")

    def bit_of(bit):
        return (me // (1 << bit)) % 2

    def start(layer):
        stage = done[layer]
        bit = halving_order(parts, layer)[stage]
        half = parts >> (stage + 1)
        mine = bit_of(bit)
        copies[layer] = remote(
            current[layer].at[pl.ds((1 - mine) * half, half)],
            landing[layer][stage],
            send_sem.at[layer, stage],
            recv_sem.at[layer, stage],
            me + (1 - 2 * mine) * (1 << bit),
        )
        copies[layer].start()

    def advance(layer):
        stage = done[layer]
        if stage == stages:
            return
        half = parts >> (stage + 1)
        mine = bit_of(halving_order(parts, layer)[stage])
        copies[layer].wait()
        source, arrived = current[layer], landing[layer][stage]
        done[layer] += 1
        if stage == stages - 1:
            total = source[mine].astype(f32) + arrived[0].astype(f32)
            if layer == 1:
                proc_out[...] = total
            elif layer == 2:
                enc_out[:, wide:side] = total
            else:
                enc_out[:, 0:wide] = total[:, 0:wide]
                enc_out[:, side:] = total[:, wide:]
            return
        target = kept[layer][stage]

        def add(k, carry):
            target[k] = (source[mine * half + k].astype(f32) + arrived[k].astype(f32)).astype(bf16)
            return carry

        lax.fori_loop(0, half, add, 0)
        current[layer] = target
        start(layer)

    prev, after, has_prev, has_next = neighbours(parts)
    greet(
        [(me + (1 - 2 * bit_of(bit)) * (1 << bit), me >= 0) for bit in range(stages)]
        + [(prev, has_prev), (after, has_next)]
    )
    rims = (rim_up, rim_down, back_lo, back_hi, rim_send, rim_recv)
    halos = (grid_hi, grid_lo, from_prev, from_next, halo_send, halo_recv)
    start_halo(parts, *rims)
    start(1)

    rows, width = latent.shape
    groups = send_slot.shape[0] // GB
    cols_r = recv_slot[...].T
    cot_ref[...] = d_latent[...]
    acc[...] = jnp.zeros_like(acc)
    d_emb_acc[...] = jnp.zeros_like(d_emb_acc)
    w0_acc[...] = jnp.zeros_like(w0_acc)
    finish_halo(parts, *rims)
    cot_ref[0:HM, :] += back_lo[...].astype(f32)
    cot_ref[rows - HM :, :] += back_hi[...].astype(f32)
    cot = cot_ref[...].astype(bf16).astype(f32)
    g, d_gain = tail_backward(mixed[...], cot, gains[0:1, :])
    d_agg = dot_tb(g, w[0, 3]).astype(bf16)
    write_shards(node_w, 0, 0, dot_ta(g, latent[...]))
    write_shards(node_w, 0, width, dot_ta(g, agg[...]))
    start(2)
    for group in range(groups):
        tile = pl.ds(group * GB * BLK, GB * BLK)
        d_send, d_recv, d_emb = edges_backward(
            group, d_agg, slopes[group * GE : (group + 1) * GE, :], cols_r, send_slot,
            recv_slot, recv_block, attr,
        )
        d_send = d_send.astype(bf16)
        d_rows[tile, :] = dot_tb(d_send, w[0, 0]).astype(bf16)
        acc[...] += d_recv
        d_emb_acc[...] += d_emb
        w0_acc[...] += dot_ta(d_send, tiles[tile, :])
        if group == 0:
            advance(1)
        if group == 1:
            advance(2)

    d_recv = acc[...].astype(bf16)
    write_shards(enc_w, 0, 0, w0_acc[...])
    write_shards(enc_w, 0, width, dot_ta(d_recv, latent[...]))
    write_small(enc_w, 0, 2 * width, d_emb_acc[...], d_gain)
    start(0)

    own = grid_grad.shape[0]
    places = row_places(send_block, send_slot.shape[0])
    ids = lax.broadcasted_iota(jnp.int32, (HG, places.shape[1]), 0)

    def scattered(chunk):
        return dot((ids + chunk * HG == places).astype(f32).astype(bf16), d_rows[...]).astype(bf16)

    def own_chunk(chunk, carry):
        grid_grad[pl.ds(pl.multiple_of(chunk * HG, HG), HG), :] = scattered(chunk + 1)
        return carry

    grid_lo[...] = scattered(0)
    grid_hi[...] = scattered(own // HG + 1)
    start_halo(parts, *halos)
    middle = own // HG // 2
    advance(1)
    advance(0)
    lax.fori_loop(0, middle, own_chunk, 0)
    advance(2)
    advance(1)
    lax.fori_loop(middle, own // HG, own_chunk, 0)
    mesh_grad[...] = (cot + dot_tb(g, w[0, 2]) + dot_tb(d_recv, w[0, 1])).astype(bf16)
    for _ in range(stages):
        advance(1)
        advance(2)
        advance(0)
    finish_halo(parts, *halos)
    grid_grad[0:HG, :] += from_prev[...]
    grid_grad[own - HG :, :] += from_next[...]


def first_exchange_kernel(
    parts, up, down, enc_a, proc_a, emb, from_prev, from_next, enc_attr, proc_attr, emb_out,
    wide, narrow, send_sem, recv_sem,
):
    prev, after, has_prev, has_next = neighbours(parts)
    greet([(prev, has_prev), (after, has_next)])
    refs = (up, down, from_prev, from_next, send_sem, recv_sem)
    start_halo(parts, *refs)

    def split(value, work, order):
        top = value.astype(bf16).astype(f32)
        rest = value - top
        work[...] = jnp.zeros_like(work)
        for k, high in enumerate(order):
            work[4 * k : 4 * k + 4, :] = top if high else rest
        return work[...].astype(bf16)

    enc_attr[...] = split(enc_a[...], wide, (1, 0, 1))
    proc_attr[...] = split(proc_a[...], wide, (1, 0, 1))
    for layer in range(2):
        emb_out[layer] = split(emb[layer], narrow, (1, 1, 0))
    finish_halo(parts, *refs)


def per_device(
    grid_latent, mesh_latent, out_cotangent, matrices, norm_gains, edge_embeddings,
    enc_attributes, proc_attributes, enc_send_block, enc_recv_block, enc_send_slot,
    enc_recv_slot, enc_count, proc_send_block, proc_recv_block, proc_send_slot,
    proc_recv_slot, proc_count,
):
    parts = lax.axis_size("space")
    rows, width = mesh_latent.shape
    own = grid_latent.shape[0]
    blocks = enc_send_block.shape[0]
    p_blocks = proc_send_block.shape[0]
    sds = jax.ShapeDtypeStruct

    edges = enc_attributes.shape[1]
    lo, hi, enc_attr, proc_attr, emb = pl.pallas_call(
        functools.partial(first_exchange_kernel, parts),
        grid=(1,),
        in_specs=[
            pl.BlockSpec((HG, width), lambda i: (own // HG - 1, 0)),
            pl.BlockSpec((HG, width), lambda i: (0, 0)),
        ]
        + [vmem] * 3,
        out_specs=[vmem] * 5,
        out_shape=[sds((HG, width), bf16)] * 2
        + [sds((16, edges), bf16)] * 2
        + [sds((2, 16, width), bf16)],
        scratch_shapes=[
            pltpu.VMEM((16, edges), f32),
            pltpu.VMEM((16, width), f32),
            pltpu.SemaphoreType.DMA((2,)),
            pltpu.SemaphoreType.DMA((2,)),
        ],
        compiler_params=pltpu.CompilerParams(
            collective_id=0, has_side_effects=True, vmem_limit_bytes=VMEM_LIMIT
        ),
    )(grid_latent, grid_latent, enc_attributes, proc_attributes, edge_embeddings)
    enc_out, agg, mixed, slopes, tiles = call(
        enc_forward_kernel,
        [smem] * 3 + [hbm] * 3 + [vmem, layer_spec(0, matrices.shape), vmem, layer_spec(0, emb.shape), vmem, vmem, vmem],
        [
            sds((rows, width), bf16),
            sds((rows, width), bf16),
            sds((rows, width), f32),
            sds((blocks * EPB, width), bf16),
            sds((blocks * BLK, width), bf16),
        ],
        [
            pltpu.VMEM((own + 2 * HG, width), bf16),
            pltpu.VMEM((rows, width), f32),
            pltpu.SemaphoreType.DMA((3,)),
        ],
        4_000_000_000,
    )(
        enc_send_block, enc_recv_block, enc_count, grid_latent, lo, hi, mesh_latent, matrices,
        norm_gains, emb, enc_attr, enc_send_slot, enc_recv_slot,
    )

    lo, hi = exchange(parts, enc_out, enc_out, width, HM, rows // HM - 1, 0, 1)
    mesh_out, d_latent, rim_lo, rim_hi, proc_w = call(
        proc_kernel,
        [smem] * 3 + [vmem] * 4 + [layer_spec(1, matrices.shape), vmem, layer_spec(1, emb.shape), vmem, vmem, vmem],
        [
            sds((rows, width), bf16),
            sds((rows, width), f32),
            sds((HM, width), bf16),
            sds((HM, width), bf16),
            sds((parts, width // parts, 4 * width + SMALL), bf16),
        ],
        [
            pltpu.VMEM((rows + 2 * HM, width), bf16),
            pltpu.VMEM((rows + 2 * HM, width), bf16),
            pltpu.VMEM((p_blocks * EPB, width), bf16),
            pltpu.VMEM((rows, width), f32),
            pltpu.VMEM((rows + 2 * HM, width), f32),
            pltpu.VMEM((16, width), f32),
        ],
        8_000_000_000,
    )(
        proc_send_block, proc_recv_block, proc_count, enc_out, lo, hi, out_cotangent, matrices,
        norm_gains, emb, proc_attr, proc_send_slot, proc_recv_slot,
    )

    stages = parts.bit_length() - 1
    columns = 4 * width + SMALL
    shard = width // parts
    streams = []
    for wide in (2 * width + SMALL, columns, 2 * width):
        landing = [pltpu.VMEM((parts >> (k + 1), shard, wide), bf16) for k in range(stages)]
        streams += landing + landing[:-1]
    mesh_grad, grid_grad, enc_sum, proc_sum = pl.pallas_call(
        functools.partial(enc_backward_kernel, parts),
        grid=(1,),
        in_specs=[smem] * 2 + [vmem] * 8 + [layer_spec(0, matrices.shape)] + [vmem] * 5,
        out_specs=[vmem] * 4,
        out_shape=[
            sds((rows, width), bf16),
            sds((own, width), bf16),
            sds((shard, columns), f32),
            sds((shard, columns), f32),
        ],
        scratch_shapes=[pltpu.VMEM((HM, width), bf16)] * 2
        + [pltpu.VMEM((HG, width), bf16)] * 4
        + [
            pltpu.VMEM((parts, shard, 2 * width + SMALL), bf16),
            pltpu.VMEM((parts, shard, 2 * width), bf16),
            pltpu.VMEM((blocks * BLK, width), bf16),
            pltpu.VMEM((rows, width), f32),
            pltpu.VMEM((16, width), f32),
            pltpu.VMEM((width, width), f32),
            pltpu.VMEM((rows, width), f32),
        ]
        + streams
        + [pltpu.SemaphoreType.DMA((2,))] * 4
        + [pltpu.SemaphoreType.DMA((3, stages))] * 2,
        compiler_params=pltpu.CompilerParams(
            collective_id=2, has_side_effects=True, vmem_limit_bytes=VMEM_LIMIT
        ),
    )(
        enc_send_block, enc_recv_block, d_latent, rim_hi, rim_lo, mesh_latent, agg, mixed, slopes,
        tiles, matrices, norm_gains, enc_attr, enc_send_slot, enc_recv_slot, proc_w,
    )

    sums = jnp.stack([enc_sum, proc_sum])
    columns = sums.shape[1]
    matrix_grads = sums[:, :, : 4 * width].reshape(2, columns, 4, width).transpose(0, 2, 3, 1)
    small = sums[:, :, 4 * width :].transpose(0, 2, 1)
    embedding_grads = small[:, 0:4] + small[:, 4:8]
    gain_grads = small[:, 16]
    return (mesh_out, grid_grad, mesh_grad, matrix_grads, gain_grads, embedding_grads)


def solution(mesh):
    rows = P(("groups", "space"), None)
    lists = (P("space"), P("space"), P("space", None), P("space", None), P("space"))
    return jax.shard_map(
        per_device,
        mesh=mesh,
        in_specs=(rows, rows, rows, P(), P(), P(), P(None, "space"), P(None, "space")) + lists + lists,
        out_specs=(
            rows,
            rows,
            rows,
            P("groups", None, None, "space"),
            P("groups", "space"),
            P("groups", None, "space"),
        ),
        check_vma=False,
    )
```
